256 devices in a mesh: patch: 256 (over x, y, z, core).
Axes of the slice: x: 4, y: 4, z: 8, core: 2. Of those that a mesh axis runs over, the one named last changes fastest.
Arguments:
- node_feats: bfloat16 [65536, 512], P('patch'), may hold values from -6 to 6
- edge_feats: bfloat16 [393216, 512], P('patch'), may hold values from -6 to 6
- senders: int32 [393216], P('patch'), may hold values from 0 to 1023, as said below
- receivers: int32 [393216], P('patch'), may hold values from 0 to 255, as said below
- halo_send: int32 [65536], P('patch'), may hold values from 0 to 255
- edge_first: bfloat16 [1536, 512], replicated, may hold values from -0.15625 to 0.15625
- edge_second: bfloat16 [512, 512], replicated, may hold values from -0.25 to 0.25
- edge_gain: float32 [512], replicated, may hold values from 0.5 to 2
- node_first: bfloat16 [1024, 512], replicated, may hold values from -0.1875 to 0.1875
- node_second: bfloat16 [512, 512], replicated, may hold values from -0.25 to 0.25
- node_gain: float32 [512], replicated, may hold values from 0.5 to 2
- node_cotangent: bfloat16 [65536, 512], P('patch'), may hold values from -6 to 6
- edge_cotangent: bfloat16 [393216, 512], P('patch'), may hold values from -6 to 6
Outputs:
- node_out: bfloat16 [65536, 512], P('patch')
- edge_out: bfloat16 [393216, 512], P('patch')
- node_grads: bfloat16 [65536, 512], P('patch')
- edge_grads: bfloat16 [393216, 512], P('patch')
The draws below stay inside these ranges and needn't reach their ends.
Inputs may be any that keep to these rules, and one draw needn't show every extreme that they name: `senders`: row of the node table of the edge's patch p: rows 0 to 255 are p's nodes; then four blocks of 64 rows, block k holding the nodes that patch (p - offset_k) mod 256 lists in its block k of halo_send, offsets (1, -1, 8, -8); then all 512 coarse nodes, coarse node c being node c % 2 of patch c // 2. Every halo row is read by some edge of its patch, and every coarse node by some edge. `receivers`: node of the edge's own patch; every node of a patch receives some edge. `halo_send`: block k of a patch's 64 entries names its nodes read by patch (p + offset_k) mod 256.
All inputs are finite; a program needn't handle non-finite values.
Results may differ from the reference program's by a relative error of at most 0.01.
Values may be sent and summed in bfloat16 or wider, within the bound.
No kernel may reach another device: no remote copies, remote signals or barrier semaphores. Data moves between devices by JAX's collectives and lax.ppermute only.
A program may use at most 128 MiB of HBM per device.

```python
import math
import jax
import jax.numpy as jnp
from jax import lax

D = 512
NODE_DEV = 256
COARSE_DEV = 2
COARSE_EDGES = 512
PATCH_COLS = 8
HALO = 64
EDGE_DEV = 1536
NODES = 65536
EDGES = 393216
N_PATCH = 256


def draw_senders(key, part):
    key = jax.random.fold_in(key, 11)
    patches = EDGES // EDGE_DEV
    middle = EDGE_DEV - COARSE_EDGES - NODE_DEV
    keys = jax.random.split(jax.random.fold_in(key, 1), patches)
    halo_part = NODE_DEV + jax.vmap(lambda one_key: jax.random.permutation(one_key, NODE_DEV))(keys).astype(jnp.int32)
    rest = jax.random.randint(jax.random.fold_in(key, 2), (patches, middle), 0, 2 * NODE_DEV, dtype=jnp.int32)
    order = jax.random.permutation(jax.random.fold_in(key, 3), patches * COARSE_EDGES).astype(jnp.int32)
    coarse = 2 * NODE_DEV + (order % (COARSE_DEV * patches)).reshape(patches, COARSE_EDGES)
    return jnp.concatenate([halo_part, rest, coarse], axis=1).reshape(EDGES).astype(jnp.int32)


def draw_receivers(key, part):
    key = jax.random.fold_in(key, 23)
    patches = EDGES // EDGE_DEV
    middle = EDGE_DEV - COARSE_EDGES - NODE_DEV
    keys = jax.random.split(jax.random.fold_in(key, 1), patches)
    leading = jax.vmap(lambda one_key: jax.random.permutation(one_key, NODE_DEV))(keys).astype(jnp.int32)
    rest = jax.random.randint(jax.random.fold_in(key, 2), (patches, middle), 0, NODE_DEV, dtype=jnp.int32)
    coarse = jax.random.randint(jax.random.fold_in(key, 3), (patches, COARSE_EDGES), 0, COARSE_DEV, dtype=jnp.int32)
    return jnp.concatenate([leading, rest, coarse], axis=1).reshape(EDGES).astype(jnp.int32)


def with_ends(values, own_key, low, high):
    shape = values.shape
    spot = [jax.random.randint(jax.random.fold_in(own_key, axis), (), 0, shape[axis]) for axis in range(len(shape))]
    values = values.at[tuple(spot)].set(low)
    longest = shape.index(max(shape))
    spot[longest] = (spot[longest] + 1) % shape[longest]
    return values.at[tuple(spot)].set(high)


def shard_levels(key, dims, cuts, low, high):
    def one(position, parts):
        steps = jax.random.uniform(jax.random.fold_in(jax.random.fold_in(key, 6), position), (parts,), jnp.float32, low / len(cuts), high / len(cuts))
        return jnp.repeat(jnp.exp(steps), dims[position] // parts).reshape((-1,) + (1,) * (len(dims) - position - 1))

    level = one(*cuts[0])
    for cut in cuts[1:]:
        level = level * one(*cut)
    return level


def normal_values(own_key, dims, deviation, reach, shards=(), held_as=jnp.bfloat16):
    result = jax.random.normal(own_key, dims, jnp.float32) * deviation
    if len(shards) > 0:
        result = shard_levels(own_key, dims, shards, -0.22, 0.18) * result
    return jnp.clip(result, min=-reach, max=reach).astype(held_as)


def setup_inputs(seed: int = 0) -> dict:
    streams_of = jax.random.split(jax.random.key(seed), 14)
    node_feats = normal_values(streams_of[0], (NODES, D), 1.0, 6.0, ((0, 256),))
    edge_feats = normal_values(streams_of[1], (EDGES, D), 1.0, 6.0, ((0, 256),))
    senders = draw_senders(jax.random.fold_in(streams_of[13], 71), 0)
    receivers = draw_receivers(jax.random.fold_in(streams_of[13], 71), 0)
    halo_send = with_ends(jax.random.randint(streams_of[4], (NODES,), 0, NODE_DEV), jax.random.fold_in(streams_of[4], 1), 0, NODE_DEV - 1).astype(jnp.int32)
    edge_first = normal_values(streams_of[5], (3 * D, D), (3 * D) ** -0.5, 0.15625)
    edge_second = normal_values(streams_of[6], (D, D), D ** -0.5, 0.25)
    edge_gain = jnp.clip(jnp.exp(jax.random.uniform(streams_of[7], (D,), jnp.float32, math.log(0.5), math.log(2.0))), 0.5, 2.0)
    node_first = normal_values(streams_of[8], (2 * D, D), (2 * D) ** -0.5, 0.1875)
    node_second = normal_values(streams_of[9], (D, D), D ** -0.5, 0.25)
    node_gain = jnp.clip(jnp.exp(jax.random.uniform(streams_of[10], (D,), jnp.float32, math.log(0.5), math.log(2.0))), 0.5, 2.0)
    node_cotangent = normal_values(streams_of[11], (NODES, D), 1.0, 6.0, ((0, 256),))
    edge_cotangent = normal_values(streams_of[12], (EDGES, D), 1.0, 6.0, ((0, 256),))
    return dict(node_feats=node_feats, edge_feats=edge_feats, senders=senders, receivers=receivers, halo_send=halo_send, edge_first=edge_first, edge_second=edge_second, edge_gain=edge_gain, node_first=node_first, node_second=node_second, node_gain=node_gain, node_cotangent=node_cotangent, edge_cotangent=edge_cotangent)


def block_forward(inputs, w_first, w_second, scale_gain):
    hidden = jnp.dot(inputs, w_first, preferred_element_type=jnp.float32)
    active = (hidden * jax.nn.sigmoid(hidden)).astype(jnp.bfloat16)
    second = jnp.dot(active, w_second, preferred_element_type=jnp.float32)
    centred = second - lax.optimization_barrier(jnp.mean(second, axis=-1, keepdims=True))
    inv_std = lax.rsqrt(lax.optimization_barrier(jnp.mean(centred * centred, axis=-1, keepdims=True)) + 1e-05)
    normed = centred * inv_std
    return (normed * scale_gain, (hidden, normed, inv_std))

def block_backward(stored, grad_out, w_first, w_second, scale_gain):
    hidden, normed, inv_std = stored
    grad_normed = grad_out * scale_gain
    grad_second = (grad_normed - lax.optimization_barrier(jnp.mean(grad_normed, axis=-1, keepdims=True)) - normed * lax.optimization_barrier(jnp.mean(grad_normed * normed, axis=-1, keepdims=True))) * inv_std
    grad_active = jnp.dot(grad_second.astype(jnp.bfloat16), w_second.T, preferred_element_type=jnp.float32)
    sigmoid_val = jax.nn.sigmoid(hidden)
    grad_hidden = (grad_active * sigmoid_val * (1.0 + hidden * (1.0 - sigmoid_val))).astype(jnp.bfloat16)
    return jnp.dot(grad_hidden, w_first.T, preferred_element_type=jnp.float32)

def reference(node_feats, edge_feats, senders, receivers, halo_send, edge_first, edge_second, edge_gain, node_first, node_second, node_gain, node_cotangent, edge_cotangent):
    device = jnp.arange(N_PATCH, dtype=jnp.int32)[:, None]
    local_rows = senders.reshape(N_PATCH, EDGE_DEV)
    send_rows = halo_send.reshape(N_PATCH, 4, HALO)
    offsets = jnp.array([1, -1, PATCH_COLS, -PATCH_COLS], dtype=jnp.int32)
    halo_slot = jnp.clip(local_rows - NODE_DEV, 0, 4 * HALO - 1)
    direction = halo_slot // HALO
    source = (device - offsets[direction]) % N_PATCH
    halo_id = source * NODE_DEV + send_rows[source, direction, halo_slot % HALO]
    coarse = jnp.clip(local_rows - 2 * NODE_DEV, 0, COARSE_DEV * N_PATCH - 1)
    coarse_id = coarse // COARSE_DEV * NODE_DEV + coarse % COARSE_DEV
    own_id = device * NODE_DEV + local_rows
    send_ids = jnp.where(local_rows < NODE_DEV, own_id, jnp.where(local_rows < 2 * NODE_DEV, halo_id, coarse_id)).reshape(-1).astype(jnp.int32)
    recv_ids = (device * NODE_DEV + receivers.reshape(N_PATCH, EDGE_DEV)).reshape(-1).astype(jnp.int32)
    edge_in = jnp.concatenate([edge_feats, node_feats[send_ids], node_feats[recv_ids]], axis=1)
    message, edge_stored = block_forward(edge_in, edge_first, edge_second, edge_gain)
    edge_out = (edge_feats.astype(jnp.float32) + message).astype(jnp.bfloat16)
    message_half = lax.optimization_barrier(message.astype(jnp.bfloat16))
    summed = jax.ops.segment_sum(message_half.astype(jnp.float32), recv_ids, num_segments=NODES).astype(jnp.bfloat16)
    update, node_stored = block_forward(jnp.concatenate([node_feats, summed], axis=1), node_first, node_second, node_gain)
    node_out = (node_feats.astype(jnp.float32) + update).astype(jnp.bfloat16)
    node_bar = node_cotangent.astype(jnp.float32)
    joined_bar = block_backward(node_stored, node_bar, node_first, node_second, node_gain)
    node_acc = node_bar + joined_bar[:, :D]
    summed_bar = joined_bar[:, D:]
    edge_bar = edge_cotangent.astype(jnp.float32)
    message_bar = edge_bar + summed_bar[recv_ids]
    edge_in_bar = block_backward(edge_stored, message_bar, edge_first, edge_second, edge_gain)
    edge_grads = (edge_bar + edge_in_bar[:, :D]).astype(jnp.bfloat16)
    node_acc = node_acc + jax.ops.segment_sum(edge_in_bar[:, D:2 * D], send_ids, num_segments=NODES)
    node_acc = node_acc + jax.ops.segment_sum(edge_in_bar[:, 2 * D:], recv_ids, num_segments=NODES)
    return (node_out, edge_out, node_acc.astype(jnp.bfloat16), edge_grads)
```

```python
import functools

import jax
import jax.numpy as jnp
from jax import lax
from jax.experimental import pallas as pl
from jax.experimental.pallas import tpu as pltpu
from jax.sharding import Mesh
from jax.sharding import PartitionSpec as P

D = 512
COARSE_DEV = 2
PATCH_COLS = 8
LANES = 128
BLOCK = 512
VMEM_LIMIT = 56 * 1024 * 1024
CHIP = ("x", "y", "z")
AXES = CHIP + ("core",)
BF = jnp.bfloat16
F32 = jnp.float32

VMEM = pl.BlockSpec(memory_space=pltpu.VMEM)
ANY = pl.BlockSpec(memory_space=pl.ANY)


def dot(a, b):
    return jnp.dot(a, b, preferred_element_type=F32)


def dot_nt(a, b):
    return lax.dot_general(a, b, (((1,), (1,)), ((), ())), preferred_element_type=F32)


def dot_tn(a, b):
    return lax.dot_general(a, b, (((0,), (0,)), ((), ())), preferred_element_type=F32)


def pick_rows(ids_row, first, count):
    shape = (count, ids_row.shape[1])
    rows = lax.broadcasted_iota(jnp.int32, shape, 0) + first
    return jnp.where(jnp.broadcast_to(ids_row, shape) == rows, 1.0, 0.0).astype(BF)


def pick_columns(ids_row, first, count):
    size = ids_row.shape[1]
    column = jnp.transpose(jnp.broadcast_to(ids_row, (LANES, size)))
    lane = lax.broadcasted_iota(jnp.int32, (size, LANES), 1) + first
    parts = [
        jnp.where(column == lane + start, 1.0, 0.0).astype(BF) for start in range(0, count, LANES)
    ]
    return jnp.concatenate(parts, axis=1) if len(parts) > 1 else parts[0]


def row_mean(value):
    return jnp.sum(value, axis=-1, keepdims=True) * (1.0 / value.shape[-1])


def normalize(second):
    centred = second - row_mean(second)
    inv_std = lax.rsqrt(row_mean(centred * centred) + 1e-05)
    return centred * inv_std, inv_std


def activate(hidden):
    sigmoid_val = jax.nn.sigmoid(hidden)
    return hidden * sigmoid_val, sigmoid_val * (1.0 + hidden * (1.0 - sigmoid_val))


def normalize_backward(grad_out, gain, normed, inv_std):
    grad_normed = grad_out * gain
    return (
        grad_normed - row_mean(grad_normed) - normed * row_mean(grad_normed * normed)
    ) * inv_std


def block_rows(step):
    return pl.ds(pl.multiple_of(step * BLOCK, BLOCK), BLOCK)


def id_row(ref, first=0, count=None):
    count = ref.shape[0] if count is None else count
    return jnp.concatenate([ref[pl.ds(first + i, 1), :] for i in range(count)], axis=1)


def block_ids(ref, step):
    return id_row(ref, step * (BLOCK // LANES), BLOCK // LANES)


def place_coarse(ids, nodes, coarse_rows):
    devices = coarse_rows // COARSE_DEV
    coarse = ids - 2 * nodes
    node, owner = jnp.bitwise_and(coarse, 1), jnp.right_shift(coarse, 1)
    core = jnp.bitwise_xor(jnp.bitwise_and(owner, 1), lax.axis_index("core"))
    place = node * devices + core * (devices // 2) + jnp.right_shift(owner, 1)
    return jnp.where(coarse < 0, ids, 2 * nodes + place)


def prepare_kernel(halo_ref, node_ref, spread_ref, *out_refs):
    size = out_refs[0].shape[0]
    rows = pick_rows(id_row(halo_ref), 0, node_ref.shape[0])
    picked = dot_tn(rows, node_ref[...]).astype(BF)
    for direction, out_ref in enumerate(out_refs):
        out_ref[...] = picked[direction * size : (direction + 1) * size]
    lead = node_ref[:16].astype(F32)
    quarters = [
        lead[node : node + 1, q * LANES : (q + 1) * LANES]
        for node in range(COARSE_DEV)
        for q in range(4)
    ]
    tile = jnp.concatenate(quarters, axis=0)
    copies = spread_ref.shape[0] // 8
    spread = jnp.broadcast_to(tile[None], (copies, 8, LANES))
    spread_ref[...] = spread.reshape(spread_ref.shape).astype(BF)


def main_kernel(
    send_ref,
    recv_ref,
    gain_ref,
    node_gain_ref,
    edge_hbm,
    cot_hbm,
    node_hbm,
    node_cot_hbm,
    halo0_hbm,
    halo1_hbm,
    halo2_hbm,
    halo3_hbm,
    coarse0_hbm,
    coarse1_hbm,
    first_hbm,
    second_hbm,
    node_first_hbm,
    node_second_hbm,
    edge_out_hbm,
    edge_grads_hbm,
    node_out_ref,
    keep_ref,
    away_ref,
    node_acc_ref,
    grad0_ref,
    grad1_ref,
    grad2_ref,
    grad3_ref,
    carry,
    edge,
    cot,
    node_ref,
    node_cot_ref,
    halo,
    coarse,
    first,
    second_ref,
    node_first_ref,
    node_second_ref,
    edge_out,
    hidden_bar,
    edge_grads,
    proj,
    stage,
    normed_all,
    inv_all,
    summed_all,
    block_sems,
    sems,
):
    blocks, nodes = cot.shape[0] // BLOCK, node_ref.shape[0]
    table = proj.shape[0] - nodes
    coarse_rows = table - 2 * nodes
    size = nodes // 4
    half = coarse.shape[0] // 2
    parity = coarse_rows // COARSE_DEV

    halo_copies = [
        pltpu.make_async_copy(source, halo.at[pl.ds(k * size, size), :], sems.at[k])
        for k, source in enumerate((halo0_hbm, halo1_hbm, halo2_hbm, halo3_hbm))
    ]
    coarse_copies = [
        pltpu.make_async_copy(source, coarse.at[pl.ds(k * half, half), :], sems.at[4 + k])
        for k, source in enumerate((coarse0_hbm, coarse1_hbm))
    ]
    first_copy = pltpu.make_async_copy(first_hbm, first, sems.at[6])
    second_copy = pltpu.make_async_copy(second_hbm, second_ref, sems.at[7])
    node_copies = [
        pltpu.make_async_copy(source, target, sems.at[8 + k])
        for k, (source, target) in enumerate(
            (
                (node_hbm, node_ref),
                (node_first_hbm, node_first_ref),
                (node_second_hbm, node_second_ref),
                (node_cot_hbm, node_cot_ref),
            )
        )
    ]

    def fetch(source, target, slot, step):
        rows = block_rows(step)
        return pltpu.make_async_copy(
            source.at[rows, :], target.at[rows, :], block_sems.at[slot, step]
        )

    edge_copy = functools.partial(fetch, edge_hbm, edge, 0)
    cot_copy = functools.partial(fetch, cot_hbm, cot, 1)
    edge_out_copy = functools.partial(fetch, edge_out, edge_out_hbm, 2)
    edge_grads_copy = functools.partial(fetch, edge_grads, edge_grads_hbm, 3)

    first_copy.start()
    node_copies[0].start()
    for copy in halo_copies + coarse_copies:
        copy.start()
    edge_copy(0).start()
    second_copy.start()
    for step in range(1, blocks):
        edge_copy(step).start()
    for copy in node_copies[1:]:
        copy.start()
    for step in range(blocks):
        cot_copy(step).start()

    first_copy.wait()
    node_copies[0].wait()
    proj[:nodes] = dot(node_ref[...], first[D : 2 * D]).astype(BF)
    proj[table:] = dot(node_ref[...], first[2 * D :]).astype(BF)
    for copy in halo_copies:
        copy.wait()
    proj[nodes : 2 * nodes] = dot(halo[...], first[D : 2 * D]).astype(BF)
    for copy in coarse_copies:
        copy.wait()
    stage[...] = coarse[...].astype(F32)
    for row in range(COARSE_DEV):
        latents = jnp.concatenate(
            [stage[pl.ds(4 * row + column, parity, 8), :] for column in range(4)], axis=1
        )
        start = 2 * nodes + row * parity
        proj[start : start + parity] = dot(latents.astype(BF), first[D : 2 * D]).astype(BF)
    summed_all[...] = jnp.zeros_like(summed_all)
    second_copy.wait()

    @pl.loop(0, blocks)
    def _(step):
        rows = block_rows(step)
        ids = place_coarse(block_ids(send_ref, step), nodes, coarse_rows)
        picks = jnp.concatenate(
            [pick_columns(ids, 0, table), pick_columns(block_ids(recv_ref, step), 0, nodes)], axis=1
        )
        edge_copy(step).wait()
        hidden = dot(edge[rows, :], first[:D]) + dot(picks, proj[...])
        active, carry[rows, :] = activate(hidden)
        normed, inv_std = normalize(dot(active.astype(BF), second_ref[...]))
        normed_all[rows, :] = normed
        inv_all[rows, :] = inv_std
        message = normed * gain_ref[...]
        summed_all[...] += dot(
            pick_rows(block_ids(recv_ref, step), 0, nodes), message.astype(BF)
        )
        edge_out[rows, :] = (edge[rows, :].astype(F32) + message).astype(BF)
        edge_out_copy(step).start()

    for copy in node_copies[1:]:
        copy.wait()
    summed = summed_all[...].astype(BF)
    node_feats = node_ref[...]
    hidden = dot(node_feats, node_first_ref[:D]) + dot(summed, node_first_ref[D:])
    active, node_slope = activate(hidden)
    normed, inv_std = normalize(dot(active.astype(BF), node_second_ref[...]))
    node_out_ref[...] = (node_feats.astype(F32) + normed * node_gain_ref[...]).astype(BF)
    node_bar = node_cot_ref[...].astype(F32)
    second_bar = normalize_backward(node_bar, node_gain_ref[...], normed, inv_std)
    active_bar = dot_nt(second_bar.astype(BF), node_second_ref[...])
    node_hidden_bar = (active_bar * node_slope).astype(BF)
    node_acc = node_bar + dot_nt(node_hidden_bar, node_first_ref[:D])
    summed_bar = dot_nt(node_hidden_bar, node_first_ref[D:]).astype(BF)

    @pl.loop(0, blocks)
    def _(step):
        rows = block_rows(step)
        cot_copy(step).wait()
        picks = pick_columns(block_ids(recv_ref, step), 0, nodes)
        message_bar = cot[rows, :].astype(F32) + dot(picks, summed_bar)
        second_bar = normalize_backward(
            message_bar, gain_ref[...], normed_all[rows, :], inv_all[rows, :]
        )
        active_bar = dot_nt(second_bar.astype(BF), second_ref[...])
        edge_hidden_bar = (active_bar * carry[rows, :]).astype(BF)
        hidden_bar[rows, :] = edge_hidden_bar
        grads = cot[rows, :].astype(F32) + dot_nt(edge_hidden_bar, first[:D])
        edge_grads[rows, :] = grads.astype(BF)
        edge_grads_copy(step).start()

    send = place_coarse(id_row(send_ref), nodes, coarse_rows)

    def sender_grads(start, count):
        sums = dot(pick_rows(send, start, count), hidden_bar[...])
        return dot_nt(sums.astype(BF), first[D : 2 * D])

    for row in range(COARSE_DEV):
        grads = sender_grads(2 * nodes + row * parity, parity)
        for column in range(4):
            stage[pl.ds(4 * row + column, parity, 8), :] = grads[
                :, column * LANES : (column + 1) * LANES
            ]
    keep_ref[...] = stage[:half]
    away_ref[...] = stage[half:].astype(BF)
    grads = sender_grads(nodes, nodes)
    for direction, grad_ref in enumerate((grad0_ref, grad1_ref, grad2_ref, grad3_ref)):
        grad_ref[...] = grads[direction * size : (direction + 1) * size].astype(BF)
    received = dot(pick_rows(id_row(recv_ref), 0, nodes), hidden_bar[...])
    node_acc += sender_grads(0, nodes) + dot_nt(received.astype(BF), first[2 * D :])
    node_acc_ref[...] = node_acc
    for step in range(blocks):
        edge_out_copy(step).wait()
        edge_grads_copy(step).wait()


def final_kernel(
    halo_ids_ref, acc_ref, back0_ref, back1_ref, back2_ref, back3_ref, parts_ref, out_ref
):
    back = jnp.concatenate(
        [back0_ref[...], back1_ref[...], back2_ref[...], back3_ref[...]], axis=0
    )
    rows = pick_rows(id_row(halo_ids_ref), 0, acc_ref.shape[0])
    acc = acc_ref[...] + dot(rows, back)
    out_ref[...] = acc.astype(BF)
    total = jnp.sum(parts_ref[...].astype(F32).reshape(-1, 8, LANES), axis=0)
    row = lax.broadcasted_iota(jnp.int32, (16, D), 0)
    lead = acc[:16]
    for node in range(COARSE_DEV):
        quarters = [total[4 * node + q : 4 * node + q + 1] for q in range(4)]
        lead += jnp.where(row == node, jnp.concatenate(quarters, axis=1), 0.0)
    out_ref[:16] = lead.astype(BF)


def call(body, outs, args, scratch=(), flops=0, specs=None, out_specs=None):
    shapes = [jax.ShapeDtypeStruct(shape, dtype) for shape, dtype in outs]
    moved = sum(a.size * a.dtype.itemsize for a in args)
    moved += sum(s.size * s.dtype.itemsize for s in shapes)
    specs, out_specs = specs or {}, out_specs or {}
    return pl.pallas_call(
        body,
        out_shape=shapes,
        in_specs=[specs.get(i, VMEM) for i in range(len(args))],
        out_specs=[out_specs.get(i, VMEM) for i in range(len(outs))],
        scratch_shapes=list(scratch),
        compiler_params=pltpu.CompilerParams(vmem_limit_bytes=VMEM_LIMIT),
        cost_estimate=pl.CostEstimate(flops=flops, bytes_accessed=moved, transcendentals=0),
    )(*args)


def shifted(value, steps):
    count = lax.axis_size(AXES)
    pairs = [(source, (source + steps) % count) for source in range(count)]
    return lax.ppermute(value, AXES, pairs)


def other_core(value):
    return lax.ppermute(value, "core", [(0, 1), (1, 0)])


def exchange(value):
    chips = lax.axis_size(CHIP)
    blocks = value.reshape(chips, 8, LANES)
    return lax.all_to_all(blocks, CHIP, 0, 0, tiled=True).reshape(chips * 8, LANES)


def shards(
    node_feats,
    edge_feats,
    senders,
    receivers,
    halo_send,
    edge_first,
    edge_second,
    edge_gain,
    node_first,
    node_second,
    node_gain,
    node_cotangent,
    edge_cotangent,
):
    nodes, edges = node_feats.shape[0], edge_feats.shape[0]
    size, blocks = nodes // 4, edges // BLOCK
    offsets = (1, -1, PATCH_COLS, -PATCH_COLS)
    devices, chips = lax.axis_size(AXES), lax.axis_size(CHIP)
    coarse_rows = COARSE_DEV * devices
    send, recv = senders.reshape(-1, LANES), receivers.reshape(-1, LANES)
    halo_ids = halo_send.reshape(-1, LANES)
    gain, node_gain = edge_gain[None], node_gain[None]

    spread, *picked = call(
        prepare_kernel,
        [((chips * 8, LANES), BF)] + [((size, D), BF)] * 4,
        (halo_ids, node_feats),
        flops=2 * nodes * nodes * D,
    )
    halos = [shifted(rows, steps) for rows, steps in zip(picked, offsets)]
    spread, *halos = lax.optimization_barrier((spread, *halos))
    coarse = exchange(spread)
    coarse_other = other_core(coarse)
    edge_out, edge_grads, node_out, keep, away, node_acc, *grads = call(
        main_kernel,
        [
            ((edges, D), BF),
            ((edges, D), BF),
            ((nodes, D), BF),
            ((chips * 8, LANES), F32),
            ((chips * 8, LANES), BF),
            ((nodes, D), F32),
        ]
        + [((size, D), BF)] * 4,
        (
            send,
            recv,
            gain,
            node_gain,
            edge_feats,
            edge_cotangent,
            node_feats,
            node_cotangent,
            *halos,
            coarse,
            coarse_other,
            edge_first,
            edge_second,
            node_first,
            node_second,
        ),
        [
            pltpu.VMEM((edges, D), F32),
            pltpu.VMEM((edges, D), BF),
            pltpu.VMEM((edges, D), BF),
            pltpu.VMEM((nodes, D), BF),
            pltpu.VMEM((nodes, D), BF),
            pltpu.VMEM((nodes, D), BF),
            pltpu.VMEM((2 * chips * 8, LANES), BF),
            pltpu.VMEM((3 * D, D), BF),
            pltpu.VMEM((D, D), BF),
            pltpu.VMEM((2 * D, D), BF),
            pltpu.VMEM((D, D), BF),
            pltpu.VMEM((edges, D), BF),
            pltpu.VMEM((edges, D), BF),
            pltpu.VMEM((edges, D), BF),
            pltpu.VMEM((3 * nodes + coarse_rows, D), BF),
            pltpu.VMEM((2 * chips * 8, LANES), F32),
            pltpu.VMEM((edges, D), F32),
            pltpu.VMEM((edges, 1), F32),
            pltpu.VMEM((nodes, D), F32),
            pltpu.SemaphoreType.DMA((4, blocks)),
            pltpu.SemaphoreType.DMA((12,)),
        ],
        flops=2 * edges * D * (2 * coarse_rows + 8 * nodes + 4 * D),
        specs={i: ANY for i in range(4, 18)},
        out_specs={0: ANY, 1: ANY},
    )
    backs = [shifted(rows, -steps) for rows, steps in zip(grads, offsets)]
    pair = (keep + other_core(away).astype(F32)).astype(BF)
    pair, *backs = lax.optimization_barrier((pair, *backs))
    parts = exchange(pair)
    (node_grads,) = call(
        final_kernel,
        [((nodes, D), BF)],
        (halo_ids, node_acc, *backs, parts),
        flops=2 * nodes * nodes * D,
    )
    return node_out, edge_out, node_grads, edge_grads


def solution(mesh):
    split = mesh.devices.reshape(-1) if mesh.devices.size != 256 else mesh.devices
    shape = (4, 4, 8, 2) if mesh.devices.size == 256 else (1, 1, 1, mesh.devices.size)
    torus = Mesh(split.reshape(shape), AXES)
    rows, vector, whole = P(AXES, None), P(AXES), P()
    in_specs = (rows, rows, vector, vector, vector) + (whole,) * 6 + (rows, rows)
    return jax.shard_map(
        shards, mesh=torus, in_specs=in_specs, out_specs=(rows,) * 4, check_vma=False
    )
```

```python
import functools

import jax
import jax.numpy as jnp
from jax import lax
from jax.experimental import pallas as pl
from jax.experimental.pallas import tpu as pltpu
from jax.sharding import Mesh
from jax.sharding import PartitionSpec as P

D = 512
COARSE_DEV = 2
PATCH_COLS = 8
LANES = 128
BLOCK = 768
STREAM = 512
VMEM_LIMIT = 56 * 1024 * 1024
CHIP = ("x", "y", "z")
AXES = CHIP + ("core",)
BF = jnp.bfloat16
F32 = jnp.float32

VMEM = pl.BlockSpec(memory_space=pltpu.VMEM)
ANY = pl.BlockSpec(memory_space=pl.ANY)


def dot(a, b):
    return jnp.dot(a, b, preferred_element_type=F32)


def dot_nt(a, b):
    return lax.dot_general(a, b, (((1,), (1,)), ((), ())), preferred_element_type=F32)


def dot_tn(a, b):
    return lax.dot_general(a, b, (((0,), (0,)), ((), ())), preferred_element_type=F32)


def pick_rows(ids_row, first, count):
    shape = (count, ids_row.shape[1])
    rows = lax.broadcasted_iota(jnp.int32, shape, 0) + first
    return jnp.where(jnp.broadcast_to(ids_row, shape) == rows, 1.0, 0.0).astype(BF)


def pick_columns(ids_row, first, count):
    size = ids_row.shape[1]
    column = jnp.transpose(jnp.broadcast_to(ids_row, (LANES, size)))
    lane = lax.broadcasted_iota(jnp.int32, (size, LANES), 1) + first
    parts = [
        jnp.where(column == lane + start, 1.0, 0.0).astype(BF) for start in range(0, count, LANES)
    ]
    return jnp.concatenate(parts, axis=1) if len(parts) > 1 else parts[0]


def row_mean(value):
    return jnp.sum(value, axis=-1, keepdims=True) * (1.0 / value.shape[-1])


def normalize(second):
    centred = second - row_mean(second)
    inv_std = lax.rsqrt(row_mean(centred * centred) + 1e-05)
    return centred * inv_std, inv_std


def activate(hidden):
    sigmoid_val = jax.nn.sigmoid(hidden)
    return hidden * sigmoid_val, sigmoid_val * (1.0 + hidden * (1.0 - sigmoid_val))


def normalize_backward(grad_out, gain, normed, inv_std):
    grad_normed = grad_out * gain
    return (
        grad_normed - row_mean(grad_normed) - normed * row_mean(grad_normed * normed)
    ) * inv_std


def block_rows(step):
    return pl.ds(pl.multiple_of(step * BLOCK, BLOCK), BLOCK)


def id_row(ref, first=0, count=None):
    count = ref.shape[0] if count is None else count
    return jnp.concatenate([ref[pl.ds(first + i, 1), :] for i in range(count)], axis=1)


def block_ids(ref, step):
    return id_row(ref, step * (BLOCK // LANES), BLOCK // LANES)


def place_coarse(ids, nodes, coarse_rows):
    devices = coarse_rows // COARSE_DEV
    coarse = ids - 2 * nodes
    node, owner = jnp.bitwise_and(coarse, 1), jnp.right_shift(coarse, 1)
    core = jnp.bitwise_xor(jnp.bitwise_and(owner, 1), lax.axis_index("core"))
    place = node * devices + core * (devices // 2) + jnp.right_shift(owner, 1)
    return jnp.where(coarse < 0, ids, 2 * nodes + place)


def neighbour_blocks():
    index = lax.axis_index("x")
    for axis in AXES[1:]:
        index = index * lax.axis_size(axis) + lax.axis_index(axis)
    core = jnp.bitwise_and(index, 1)
    row = jnp.bitwise_and(index // PATCH_COLS, 1)
    return (3 - row, 2 + row, 1 - core, core), (2 + row, 3 - row, core, 1 - core)


def block_at(block, size):
    return pl.ds(pl.multiple_of(block * size, size), size)


def halo_kernel(halo_ref, node_ref, out0_ref, out1_ref, out2_ref, out3_ref, picked):
    size = out0_ref.shape[0]
    rows = pick_rows(id_row(halo_ref), 0, node_ref.shape[0])
    picked[...] = dot_tn(rows, node_ref[...]).astype(BF)
    for block, out_ref in zip(neighbour_blocks()[0], (out0_ref, out1_ref, out2_ref, out3_ref)):
        out_ref[...] = picked[block_at(block, size)]


def partial_kernel(send_ref, recv_ref, edge_ref, node_ref, first_ref, out_ref, proj):
    nodes = node_ref.shape[0]
    step = pl.program_id(0)

    @pl.when(step == 0)
    def _():
        proj[:nodes] = dot(node_ref[...], first_ref[D : 2 * D]).astype(BF)
        proj[nodes:] = dot(node_ref[...], first_ref[2 * D :]).astype(BF)

    groups = STREAM // LANES
    picks = jnp.concatenate(
        [
            pick_columns(id_row(send_ref, step * groups, groups), 0, nodes),
            pick_columns(id_row(recv_ref, step * groups, groups), 0, nodes),
        ],
        axis=1,
    )
    out_ref[...] = dot(edge_ref[...], first_ref[:D]) + dot(picks, proj[...])


def main_kernel(
    send_ref,
    recv_ref,
    gain_ref,
    node_gain_ref,
    partial_hbm,
    edge_hbm,
    cot_hbm,
    node_hbm,
    node_cot_hbm,
    halo0_hbm,
    halo1_hbm,
    halo2_hbm,
    halo3_hbm,
    coarse0_hbm,
    coarse1_hbm,
    first_hbm,
    second_hbm,
    node_first_hbm,
    node_second_hbm,
    edge_out_hbm,
    hidden_bar_hbm,
    node_out_ref,
    keep_ref,
    away_ref,
    node_acc_ref,
    grad0_ref,
    grad1_ref,
    grad2_ref,
    grad3_ref,
    carry,
    edge,
    cot,
    node_ref,
    node_cot_ref,
    halo,
    coarse,
    first,
    second_ref,
    node_first_ref,
    node_second_ref,
    edge_out,
    hidden_bar,
    proj,
    stage,
    normed_all,
    inv_all,
    summed_all,
    block_sems,
    sems,
):
    blocks, nodes = cot.shape[0] // BLOCK, node_ref.shape[0]
    table = proj.shape[0]
    coarse_rows = table - nodes
    size = nodes // 4
    received_blocks = neighbour_blocks()[1]
    half = coarse.shape[0] // 2
    parity = coarse_rows // COARSE_DEV

    halo_copies = [
        pltpu.make_async_copy(source, halo.at[block_at(block, size), :], sems.at[k])
        for k, (block, source) in enumerate(
            zip(received_blocks, (halo0_hbm, halo1_hbm, halo2_hbm, halo3_hbm))
        )
    ]
    coarse_copies = [
        pltpu.make_async_copy(source, coarse.at[pl.ds(k * half, half), :], sems.at[4 + k])
        for k, source in enumerate((coarse0_hbm, coarse1_hbm))
    ]
    first_copy = pltpu.make_async_copy(first_hbm.at[pl.ds(D, 2 * D), :], first, sems.at[6])
    second_copy = pltpu.make_async_copy(second_hbm, second_ref, sems.at[7])
    node_copies = [
        pltpu.make_async_copy(source, target, sems.at[8 + k])
        for k, (source, target) in enumerate(
            (
                (node_hbm, node_ref),
                (node_first_hbm, node_first_ref),
                (node_second_hbm, node_second_ref),
                (node_cot_hbm, node_cot_ref),
            )
        )
    ]

    def fetch(source, target, slot, step):
        rows = block_rows(step)
        return pltpu.make_async_copy(
            source.at[rows, :], target.at[rows, :], block_sems.at[slot, step]
        )

    edge_copy = functools.partial(fetch, edge_hbm, edge, 0)
    cot_copy = functools.partial(fetch, cot_hbm, cot, 1)
    edge_out_copy = functools.partial(fetch, edge_out, edge_out_hbm, 2)
    hidden_bar_copy = functools.partial(fetch, hidden_bar, hidden_bar_hbm, 3)
    carry_copy = functools.partial(fetch, partial_hbm, carry, 4)

    first_copy.start()
    for copy in halo_copies + coarse_copies:
        copy.start()
    carry_copy(0).start()
    second_copy.start()
    edge_copy(0).start()
    for step in range(1, blocks):
        carry_copy(step).start()
        edge_copy(step).start()
    for copy in node_copies:
        copy.start()
    for step in range(blocks):
        cot_copy(step).start()

    first_copy.wait()
    for copy in halo_copies:
        copy.wait()
    proj[:nodes] = dot(halo[...], first[:D]).astype(BF)
    for copy in coarse_copies:
        copy.wait()
    stage[...] = coarse[...].astype(F32)
    for row in range(COARSE_DEV):
        latents = jnp.concatenate(
            [stage[pl.ds(4 * row + column, parity, 8), :] for column in range(4)], axis=1
        )
        start = nodes + row * parity
        proj[start : start + parity] = dot(latents.astype(BF), first[:D]).astype(BF)
    summed_all[...] = jnp.zeros_like(summed_all)
    second_copy.wait()

    @pl.loop(0, blocks, unroll=True)
    def _(step):
        rows = block_rows(step)
        ids = place_coarse(block_ids(send_ref, step), nodes, coarse_rows)
        picks = pick_columns(ids, nodes, table)
        carry_copy(step).wait()
        hidden = carry[rows, :] + dot(picks, proj[...])
        active, carry[rows, :] = activate(hidden)
        normed, inv_std = normalize(dot(active.astype(BF), second_ref[...]))
        normed_all[rows, :] = normed
        inv_all[rows, :] = inv_std
        message = normed * gain_ref[...]
        summed_all[...] += dot(
            pick_rows(block_ids(recv_ref, step), 0, nodes), message.astype(BF)
        )
        edge_copy(step).wait()
        edge_out[rows, :] = (edge[rows, :].astype(F32) + message).astype(BF)
        edge_out_copy(step).start()

    for copy in node_copies:
        copy.wait()
    summed = summed_all[...].astype(BF)
    node_feats = node_ref[...]
    hidden = dot(node_feats, node_first_ref[:D]) + dot(summed, node_first_ref[D:])
    active, node_slope = activate(hidden)
    normed, inv_std = normalize(dot(active.astype(BF), node_second_ref[...]))
    node_out_ref[...] = (node_feats.astype(F32) + normed * node_gain_ref[...]).astype(BF)
    node_bar = node_cot_ref[...].astype(F32)
    second_bar = normalize_backward(node_bar, node_gain_ref[...], normed, inv_std)
    active_bar = dot_nt(second_bar.astype(BF), node_second_ref[...])
    node_hidden_bar = (active_bar * node_slope).astype(BF)
    node_acc = node_bar + dot_nt(node_hidden_bar, node_first_ref[:D])
    summed_bar = dot_nt(node_hidden_bar, node_first_ref[D:]).astype(BF)

    @pl.loop(0, blocks, unroll=True)
    def _(step):
        rows = block_rows(step)
        cot_copy(step).wait()
        picks = pick_columns(block_ids(recv_ref, step), 0, nodes)
        message_bar = cot[rows, :].astype(F32) + dot(picks, summed_bar)
        second_bar = normalize_backward(
            message_bar, gain_ref[...], normed_all[rows, :], inv_all[rows, :]
        )
        active_bar = dot_nt(second_bar.astype(BF), second_ref[...])
        hidden_bar[rows, :] = (active_bar * carry[rows, :]).astype(BF)
        hidden_bar_copy(step).start()

    send = place_coarse(id_row(send_ref), nodes, coarse_rows)

    def sender_grads(start, count):
        sums = dot(pick_rows(send, start, count), hidden_bar[...])
        return dot_nt(sums.astype(BF), first[:D])

    for row in range(COARSE_DEV):
        grads = sender_grads(2 * nodes + row * parity, parity)
        for column in range(4):
            stage[pl.ds(4 * row + column, parity, 8), :] = grads[
                :, column * LANES : (column + 1) * LANES
            ]
    keep_ref[...] = stage[:half].astype(BF)
    away_ref[...] = stage[half:].astype(BF)
    halo[...] = sender_grads(nodes, nodes).astype(BF)
    for block, grad_ref in zip(received_blocks, (grad0_ref, grad1_ref, grad2_ref, grad3_ref)):
        grad_ref[...] = halo[block_at(block, size)]
    received = dot(pick_rows(id_row(recv_ref), 0, nodes), hidden_bar[...])
    node_acc += sender_grads(0, nodes) + dot_nt(received.astype(BF), first[D:])
    node_acc_ref[...] = node_acc
    for step in range(blocks):
        edge_out_copy(step).wait()
        hidden_bar_copy(step).wait()


def edge_grads_kernel(hidden_bar_ref, cot_ref, first_ref, out_ref):
    grad = dot_nt(hidden_bar_ref[...], first_ref[...])
    out_ref[...] = (cot_ref[...].astype(F32) + grad).astype(BF)


def final_kernel(
    halo_ids_ref, acc_ref, back0_ref, back1_ref, back2_ref, back3_ref, parts_ref, out_ref, back
):
    backs = (back0_ref, back1_ref, back2_ref, back3_ref)
    for block, back_ref in zip(neighbour_blocks()[0], backs):
        back[block_at(block, back_ref.shape[0])] = back_ref[...]
    rows = pick_rows(id_row(halo_ids_ref), 0, acc_ref.shape[0])
    acc = acc_ref[...] + dot(rows, back[...])
    out_ref[...] = acc.astype(BF)
    total = jnp.sum(parts_ref[...].astype(F32).reshape(-1, 8, LANES), axis=0)
    row = lax.broadcasted_iota(jnp.int32, (16, D), 0)
    lead = acc[:16]
    for node in range(COARSE_DEV):
        quarters = [total[4 * node + q : 4 * node + q + 1] for q in range(4)]
        lead += jnp.where(row == node, jnp.concatenate(quarters, axis=1), 0.0)
    out_ref[:16] = lead.astype(BF)


def call(body, outs, args, scratch=(), flops=0, specs=None, out_specs=None, grid=()):
    shapes = [jax.ShapeDtypeStruct(shape, dtype) for shape, dtype in outs]
    moved = sum(a.size * a.dtype.itemsize for a in args)
    moved += sum(s.size * s.dtype.itemsize for s in shapes)
    specs, out_specs = specs or {}, out_specs or {}
    return pl.pallas_call(
        body,
        out_shape=shapes,
        grid=grid,
        in_specs=[specs.get(i, VMEM) for i in range(len(args))],
        out_specs=[out_specs.get(i, VMEM) for i in range(len(outs))],
        scratch_shapes=list(scratch),
        compiler_params=pltpu.CompilerParams(vmem_limit_bytes=VMEM_LIMIT),
        cost_estimate=pl.CostEstimate(flops=flops, bytes_accessed=moved, transcendentals=0),
    )(*args)


def trade(blocks):
    count = lax.axis_size(AXES)
    arrived = []
    for block, (step, forward) in zip(blocks, ((PATCH_COLS, 0), (PATCH_COLS, 1), (1, 0), (1, 1))):
        pairs = [
            (p, (p + (step if p // step % 2 != forward else -step)) % count) for p in range(count)
        ]
        arrived.append(lax.ppermute(block, AXES, pairs))
    return arrived


def other_core(value):
    return lax.ppermute(value, "core", [(0, 1), (1, 0)])


def exchange(value):
    chips = lax.axis_size(CHIP)
    blocks = value.reshape(chips, 8, LANES)
    return lax.all_to_all(blocks, CHIP, 0, 0, tiled=True).reshape(chips * 8, LANES)


def shards(
    node_feats,
    edge_feats,
    senders,
    receivers,
    halo_send,
    edge_first,
    edge_second,
    edge_gain,
    node_first,
    node_second,
    node_gain,
    node_cotangent,
    edge_cotangent,
):
    nodes, edges = node_feats.shape[0], edge_feats.shape[0]
    size, blocks = nodes // 4, edges // BLOCK
    devices, chips = lax.axis_size(AXES), lax.axis_size(CHIP)
    coarse_rows = COARSE_DEV * devices
    send, recv = senders.reshape(-1, LANES), receivers.reshape(-1, LANES)
    halo_ids = halo_send.reshape(-1, LANES)
    gain, node_gain = edge_gain[None], node_gain[None]
    stream = pl.BlockSpec((STREAM, D), lambda i: (i, 0))

    lead = node_feats[:COARSE_DEV].reshape(1, 8, LANES)
    coarse = exchange(jnp.broadcast_to(lead, (chips, 8, LANES)))
    picked = call(
        halo_kernel,
        [((size, D), BF)] * 4,
        (halo_ids, node_feats),
        [pltpu.VMEM((nodes, D), BF)],
        flops=2 * nodes * nodes * D,
    )
    halos = trade(picked)
    (partial,) = call(
        partial_kernel,
        [((edges, D), F32)],
        (send, recv, edge_feats, node_feats, edge_first),
        [pltpu.VMEM((2 * nodes, D), BF)],
        flops=2 * edges * D * (D + 2 * nodes),
        specs={2: stream},
        out_specs={0: stream},
        grid=(edges // STREAM,),
    )
    coarse, partial, *halos = lax.optimization_barrier((coarse, partial, *halos))
    coarse_other = other_core(coarse)
    edge_out, hidden_bar, node_out, keep, away, node_acc, *grads = call(
        main_kernel,
        [
            ((edges, D), BF),
            ((edges, D), BF),
            ((nodes, D), BF),
            ((chips * 8, LANES), BF),
            ((chips * 8, LANES), BF),
            ((nodes, D), F32),
        ]
        + [((size, D), BF)] * 4,
        (
            send,
            recv,
            gain,
            node_gain,
            partial,
            edge_feats,
            edge_cotangent,
            node_feats,
            node_cotangent,
            *halos,
            coarse,
            coarse_other,
            edge_first,
            edge_second,
            node_first,
            node_second,
        ),
        [
            pltpu.VMEM((edges, D), F32),
            pltpu.VMEM((edges, D), BF),
            pltpu.VMEM((edges, D), BF),
            pltpu.VMEM((nodes, D), BF),
            pltpu.VMEM((nodes, D), BF),
            pltpu.VMEM((nodes, D), BF),
            pltpu.VMEM((2 * chips * 8, LANES), BF),
            pltpu.VMEM((2 * D, D), BF),
            pltpu.VMEM((D, D), BF),
            pltpu.VMEM((2 * D, D), BF),
            pltpu.VMEM((D, D), BF),
            pltpu.VMEM((edges, D), BF),
            pltpu.VMEM((edges, D), BF),
            pltpu.VMEM((nodes + coarse_rows, D), BF),
            pltpu.VMEM((2 * chips * 8, LANES), F32),
            pltpu.VMEM((edges, D), F32),
            pltpu.VMEM((edges, 1), F32),
            pltpu.VMEM((nodes, D), F32),
            pltpu.SemaphoreType.DMA((5, blocks)),
            pltpu.SemaphoreType.DMA((12,)),
        ],
        flops=2 * edges * D * (2 * coarse_rows + 5 * nodes + 2 * D),
        specs={i: ANY for i in range(4, 19)},
        out_specs={0: ANY, 1: ANY},
    )
    (edge_grads,) = call(
        edge_grads_kernel,
        [((edges, D), BF)],
        (hidden_bar, edge_cotangent, edge_first),
        flops=2 * edges * D * D,
        specs={0: stream, 1: stream, 2: pl.BlockSpec((D, D), lambda i: (0, 0))},
        out_specs={0: stream},
        grid=(edges // STREAM,),
    )
    backs = trade(grads)
    pair = (keep.astype(F32) + other_core(away).astype(F32)).astype(BF)
    parts = exchange(pair)
    parts, *backs = lax.optimization_barrier((parts, *backs))
    (node_grads,) = call(
        final_kernel,
        [((nodes, D), BF)],
        (halo_ids, node_acc, *backs, parts),
        [pltpu.VMEM((nodes, D), BF)],
        flops=2 * nodes * nodes * D,
    )
    return node_out, edge_out, node_grads, edge_grads


def solution(mesh):
    split = mesh.devices.reshape(-1) if mesh.devices.size != 256 else mesh.devices
    shape = (4, 4, 8, 2) if mesh.devices.size == 256 else (1, 1, 1, mesh.devices.size)
    torus = Mesh(split.reshape(shape), AXES)
    rows, vector, whole = P(AXES, None), P(AXES), P()
    in_specs = (rows, rows, vector, vector, vector) + (whole,) * 6 + (rows, rows)
    return jax.shard_map(
        shards, mesh=torus, in_specs=in_specs, out_specs=(rows,) * 4, check_vma=False
    )
```

```python
import functools

import jax
import jax.numpy as jnp
from jax import lax
from jax.experimental import pallas as pl
from jax.experimental.pallas import tpu as pltpu
from jax.sharding import Mesh
from jax.sharding import PartitionSpec as P

D = 512
COARSE_DEV = 2
PATCH_COLS = 8
LANES = 128
BLOCK = 768
STREAM = 512
PARTS = 2
VMEM_LIMIT = 56 * 1024 * 1024
FINAL_LIMIT = 8 * 1024 * 1024
CHIP = ("x", "y", "z")
AXES = CHIP + ("core",)
BF = jnp.bfloat16
F32 = jnp.float32

VMEM = pl.BlockSpec(memory_space=pltpu.VMEM)
ANY = pl.BlockSpec(memory_space=pl.ANY)


def dot(a, b):
    return jnp.dot(a, b, preferred_element_type=F32)


def dot_nt(a, b):
    return lax.dot_general(a, b, (((1,), (1,)), ((), ())), preferred_element_type=F32)


def dot_tn(a, b):
    return lax.dot_general(a, b, (((0,), (0,)), ((), ())), preferred_element_type=F32)


def pick_rows(ids_row, first, count):
    shape = (count, ids_row.shape[1])
    rows = lax.broadcasted_iota(jnp.int32, shape, 0) + first
    return jnp.where(jnp.broadcast_to(ids_row, shape) == rows, 1.0, 0.0).astype(BF)


def pick_columns(ids_row, first, count):
    size = ids_row.shape[1]
    column = jnp.transpose(jnp.broadcast_to(ids_row, (LANES, size)))
    lane = lax.broadcasted_iota(jnp.int32, (size, LANES), 1) + first
    parts = [
        jnp.where(column == lane + start, 1.0, 0.0).astype(BF) for start in range(0, count, LANES)
    ]
    return jnp.concatenate(parts, axis=1) if len(parts) > 1 else parts[0]


def row_mean(value):
    return jnp.sum(value, axis=-1, keepdims=True) * (1.0 / value.shape[-1])


def normalize(second):
    centred = second - row_mean(second)
    inv_std = lax.rsqrt(row_mean(centred * centred) + 1e-05)
    return centred * inv_std, inv_std


def activate(hidden):
    sigmoid_val = jax.nn.sigmoid(hidden)
    return hidden * sigmoid_val, sigmoid_val * (1.0 + hidden * (1.0 - sigmoid_val))


def normalize_backward(grad_out, gain, normed, inv_std):
    grad_normed = grad_out * gain
    return (
        grad_normed - row_mean(grad_normed) - normed * row_mean(grad_normed * normed)
    ) * inv_std


def block_rows(step):
    return pl.ds(pl.multiple_of(step * BLOCK, BLOCK), BLOCK)


def id_row(ref, first=0, count=None):
    count = ref.shape[0] if count is None else count
    return jnp.concatenate([ref[pl.ds(first + i, 1), :] for i in range(count)], axis=1)


def block_ids(ref, step):
    return id_row(ref, step * (BLOCK // LANES), BLOCK // LANES)


def place_coarse(ids, nodes, coarse_rows):
    devices = coarse_rows // COARSE_DEV
    coarse = ids - 2 * nodes
    node, owner = jnp.bitwise_and(coarse, 1), jnp.right_shift(coarse, 1)
    core = jnp.bitwise_xor(jnp.bitwise_and(owner, 1), lax.axis_index("core"))
    place = node * devices + core * (devices // 2) + jnp.right_shift(owner, 1)
    return jnp.where(coarse < 0, ids, 2 * nodes + place)


def neighbour_blocks():
    index = lax.axis_index("x")
    for axis in AXES[1:]:
        index = index * lax.axis_size(axis) + lax.axis_index(axis)
    core = jnp.bitwise_and(index, 1)
    row = jnp.bitwise_and(index // PATCH_COLS, 1)
    return (3 - row, 2 + row, 1 - core, core), (2 + row, 3 - row, core, 1 - core)


def block_at(block, size):
    return pl.ds(pl.multiple_of(block * size, size), size)


def prepare_kernel(halo_ref, node_ref, spread_ref, out0_ref, out1_ref, out2_ref, out3_ref, picked):
    size = out0_ref.shape[0]
    rows = pick_rows(id_row(halo_ref), 0, node_ref.shape[0])
    picked[...] = dot_tn(rows, node_ref[...]).astype(BF)
    for block, out_ref in zip(neighbour_blocks()[0], (out0_ref, out1_ref, out2_ref, out3_ref)):
        out_ref[...] = picked[block_at(block, size)]
    lead = node_ref[:16].astype(F32)
    quarters = [
        lead[node : node + 1, q * LANES : (q + 1) * LANES]
        for node in range(COARSE_DEV)
        for q in range(4)
    ]
    tile = jnp.concatenate(quarters, axis=0)
    copies = spread_ref.shape[0] // 8
    spread = jnp.broadcast_to(tile[None], (copies, 8, LANES))
    spread_ref[...] = spread.reshape(spread_ref.shape).astype(BF)


def stream_rows(step, part=0, parts=1):
    size = STREAM // parts
    return pl.ds(step * STREAM + part * size, size)


def partial_kernel(
    send_ref,
    recv_ref,
    edge_hbm,
    node_hbm,
    first_hbm,
    out_hbm,
    edge,
    node_ref,
    first,
    out,
    proj,
    sems,
    edge_sems,
    out_sems,
):
    nodes, blocks = node_ref.shape[0], edge.shape[0] // STREAM
    first_copies = [
        pltpu.make_async_copy(
            first_hbm.at[pl.ds(k * D, D), :], first.at[pl.ds(k * D, D), :], sems.at[k]
        )
        for k in range(3)
    ]
    node_copy = pltpu.make_async_copy(node_hbm, node_ref, sems.at[3])
    edge_copies = [
        pltpu.make_async_copy(
            edge_hbm.at[stream_rows(b), :], edge.at[stream_rows(b), :], edge_sems.at[b]
        )
        for b in range(blocks)
    ]
    out_copies = [
        pltpu.make_async_copy(
            out.at[stream_rows(b, p, PARTS), :],
            out_hbm.at[stream_rows(b, p, PARTS), :],
            out_sems.at[b, p],
        )
        for b in range(blocks)
        for p in range(PARTS)
    ]
    first_copies[0].start()
    edge_copies[0].start()
    node_copy.start()
    for k in (1, 2):
        first_copies[k].start()
    for copy in edge_copies[1:]:
        copy.start()
    first_copies[0].wait()
    edge_copies[0].wait()
    out[stream_rows(0), :] = dot(edge[stream_rows(0), :], first[:D])
    node_copy.wait()
    first_copies[1].wait()
    proj[:nodes] = dot(node_ref[...], first[D : 2 * D]).astype(BF)
    first_copies[2].wait()
    proj[nodes:] = dot(node_ref[...], first[2 * D :]).astype(BF)
    groups = STREAM // LANES
    for b in range(blocks):
        rows = stream_rows(b)
        picks = jnp.concatenate(
            [
                pick_columns(id_row(send_ref, b * groups, groups), 0, nodes),
                pick_columns(id_row(recv_ref, b * groups, groups), 0, nodes),
            ],
            axis=1,
        )
        if b == 0:
            out[rows, :] += dot(picks, proj[...])
        else:
            edge_copies[b].wait()
            out[rows, :] = dot(edge[rows, :], first[:D]) + dot(picks, proj[...])
        for copy in out_copies[b * PARTS : (b + 1) * PARTS]:
            copy.start()
    for copy in out_copies:
        copy.wait()


def main_kernel(
    send_ref,
    recv_ref,
    gain_ref,
    node_gain_ref,
    partial_hbm,
    edge_hbm,
    cot_hbm,
    node_hbm,
    node_cot_hbm,
    halo0_hbm,
    halo1_hbm,
    halo2_hbm,
    halo3_hbm,
    coarse0_hbm,
    coarse1_hbm,
    first_hbm,
    second_hbm,
    node_first_hbm,
    node_second_hbm,
    edge_out_hbm,
    hidden_bar_hbm,
    node_out_ref,
    keep_ref,
    away_ref,
    node_acc_ref,
    grad0_ref,
    grad1_ref,
    grad2_ref,
    grad3_ref,
    carry,
    edge,
    cot,
    node_ref,
    node_cot_ref,
    halo,
    coarse,
    first,
    second_ref,
    node_first_ref,
    node_second_ref,
    edge_out,
    hidden_bar,
    proj,
    stage,
    normed_all,
    inv_all,
    summed_all,
    block_sems,
    sems,
):
    blocks, nodes = cot.shape[0] // BLOCK, node_ref.shape[0]
    table = proj.shape[0]
    coarse_rows = table - nodes
    size = nodes // 4
    received_blocks = neighbour_blocks()[1]
    half = coarse.shape[0] // 2
    parity = coarse_rows // COARSE_DEV

    halo_copies = [
        pltpu.make_async_copy(source, halo.at[block_at(block, size), :], sems.at[k])
        for k, (block, source) in enumerate(
            zip(received_blocks, (halo0_hbm, halo1_hbm, halo2_hbm, halo3_hbm))
        )
    ]
    coarse_copies = [
        pltpu.make_async_copy(source, coarse.at[pl.ds(k * half, half), :], sems.at[4 + k])
        for k, source in enumerate((coarse0_hbm, coarse1_hbm))
    ]
    first_copy, last_copy = [
        pltpu.make_async_copy(
            first_hbm.at[pl.ds((k + 1) * D, D), :], first.at[pl.ds(k * D, D), :], sems.at[slot]
        )
        for k, slot in ((0, 6), (1, 12))
    ]
    second_copy = pltpu.make_async_copy(second_hbm, second_ref, sems.at[7])
    node_copies = [
        pltpu.make_async_copy(source, target, sems.at[8 + k])
        for k, (source, target) in enumerate(
            (
                (node_hbm, node_ref),
                (node_first_hbm, node_first_ref),
                (node_second_hbm, node_second_ref),
                (node_cot_hbm, node_cot_ref),
            )
        )
    ]

    def fetch(source, target, slot, step):
        rows = block_rows(step)
        return pltpu.make_async_copy(
            source.at[rows, :], target.at[rows, :], block_sems.at[slot, step]
        )

    edge_copy = functools.partial(fetch, edge_hbm, edge, 0)
    cot_copy = functools.partial(fetch, cot_hbm, cot, 1)
    edge_out_copy = functools.partial(fetch, edge_out, edge_out_hbm, 2)
    hidden_bar_copy = functools.partial(fetch, hidden_bar, hidden_bar_hbm, 3)
    carry_copy = functools.partial(fetch, partial_hbm, carry, 4)

    first_copy.start()
    for copy in halo_copies + coarse_copies:
        copy.start()
    carry_copy(0).start()
    second_copy.start()
    edge_copy(0).start()
    for step in range(1, blocks):
        carry_copy(step).start()
        edge_copy(step).start()
    for copy in node_copies:
        copy.start()
    for step in range(blocks):
        cot_copy(step).start()
    last_copy.start()

    first_copy.wait()
    for copy in halo_copies:
        copy.wait()
    proj[:nodes] = dot(halo[...], first[:D]).astype(BF)
    for copy in coarse_copies:
        copy.wait()
    stage[...] = coarse[...].astype(F32)
    for row in range(COARSE_DEV):
        latents = jnp.concatenate(
            [stage[pl.ds(4 * row + column, parity, 8), :] for column in range(4)], axis=1
        )
        start = nodes + row * parity
        proj[start : start + parity] = dot(latents.astype(BF), first[:D]).astype(BF)
    summed_all[...] = jnp.zeros_like(summed_all)
    second_copy.wait()

    @pl.loop(0, blocks, unroll=True)
    def _(step):
        rows = block_rows(step)
        ids = place_coarse(block_ids(send_ref, step), nodes, coarse_rows)
        picks = pick_columns(ids, nodes, table)
        normed_all[rows, :] = dot(picks, proj[...])
        carry_copy(step).wait()
        hidden = carry[rows, :] + normed_all[rows, :]
        active, carry[rows, :] = activate(hidden)
        normed, inv_std = normalize(dot(active.astype(BF), second_ref[...]))
        normed_all[rows, :] = normed
        inv_all[rows, :] = inv_std
        message = normed * gain_ref[...]
        summed_all[...] += dot(
            pick_rows(block_ids(recv_ref, step), 0, nodes), message.astype(BF)
        )
        edge_copy(step).wait()
        edge_out[rows, :] = (edge[rows, :].astype(F32) + message).astype(BF)
        edge_out_copy(step).start()

    for copy in node_copies:
        copy.wait()
    summed = summed_all[...].astype(BF)
    node_feats = node_ref[...]
    hidden = dot(node_feats, node_first_ref[:D]) + dot(summed, node_first_ref[D:])
    active, node_slope = activate(hidden)
    normed, inv_std = normalize(dot(active.astype(BF), node_second_ref[...]))
    node_out_ref[...] = (node_feats.astype(F32) + normed * node_gain_ref[...]).astype(BF)
    node_bar = node_cot_ref[...].astype(F32)
    second_bar = normalize_backward(node_bar, node_gain_ref[...], normed, inv_std)
    active_bar = dot_nt(second_bar.astype(BF), node_second_ref[...])
    node_hidden_bar = (active_bar * node_slope).astype(BF)
    node_acc = node_bar + dot_nt(node_hidden_bar, node_first_ref[:D])
    summed_bar = dot_nt(node_hidden_bar, node_first_ref[D:]).astype(BF)

    @pl.loop(0, blocks, unroll=True)
    def _(step):
        rows = block_rows(step)
        cot_copy(step).wait()
        picks = pick_columns(block_ids(recv_ref, step), 0, nodes)
        message_bar = cot[rows, :].astype(F32) + dot(picks, summed_bar)
        second_bar = normalize_backward(
            message_bar, gain_ref[...], normed_all[rows, :], inv_all[rows, :]
        )
        active_bar = dot_nt(second_bar.astype(BF), second_ref[...])
        hidden_bar[rows, :] = (active_bar * carry[rows, :]).astype(BF)
        hidden_bar_copy(step).start()

    send = place_coarse(id_row(send_ref), nodes, coarse_rows)

    def sender_grads(start, count):
        sums = dot(pick_rows(send, start, count), hidden_bar[...])
        return dot_nt(sums.astype(BF), first[:D])

    for row in range(COARSE_DEV):
        grads = sender_grads(2 * nodes + row * parity, parity)
        for column in range(4):
            stage[pl.ds(4 * row + column, parity, 8), :] = grads[
                :, column * LANES : (column + 1) * LANES
            ]
    keep_ref[...] = stage[:half].astype(BF)
    away_ref[...] = stage[half:].astype(BF)
    halo[...] = sender_grads(nodes, nodes).astype(BF)
    for block, grad_ref in zip(received_blocks, (grad0_ref, grad1_ref, grad2_ref, grad3_ref)):
        grad_ref[...] = halo[block_at(block, size)]
    last_copy.wait()
    received = dot(pick_rows(id_row(recv_ref), 0, nodes), hidden_bar[...])
    node_acc += sender_grads(0, nodes) + dot_nt(received.astype(BF), first[D:])
    node_acc_ref[...] = node_acc
    for step in range(blocks):
        edge_out_copy(step).wait()
        hidden_bar_copy(step).wait()


def edge_grads_kernel(
    hidden_bar_hbm, cot_hbm, first_hbm, out_hbm, hidden_bar, cot, first, out, sem, in_sems, out_sems
):
    blocks = out.shape[0] // STREAM
    first_copy = pltpu.make_async_copy(first_hbm.at[pl.ds(0, D), :], first, sem.at[0])
    in_copies = [
        [
            pltpu.make_async_copy(
                source.at[stream_rows(b), :], target.at[stream_rows(b), :], in_sems.at[b, k]
            )
            for k, (source, target) in enumerate(((hidden_bar_hbm, hidden_bar), (cot_hbm, cot)))
        ]
        for b in range(blocks)
    ]
    out_copies = [
        pltpu.make_async_copy(
            out.at[stream_rows(b, p, PARTS), :],
            out_hbm.at[stream_rows(b, p, PARTS), :],
            out_sems.at[b, p],
        )
        for b in range(blocks)
        for p in range(PARTS)
    ]
    first_copy.start()
    for pair in in_copies:
        for copy in pair:
            copy.start()
    first_copy.wait()
    for b in range(blocks):
        rows = stream_rows(b)
        for copy in in_copies[b]:
            copy.wait()
        grad = dot_nt(hidden_bar[rows, :], first[...])
        out[rows, :] = (cot[rows, :].astype(F32) + grad).astype(BF)
        for copy in out_copies[b * PARTS : (b + 1) * PARTS]:
            copy.start()
    for copy in out_copies:
        copy.wait()


def final_kernel(
    halo_ids_ref, acc_ref, back0_ref, back1_ref, back2_ref, back3_ref, parts_ref, out_ref, back
):
    backs = (back0_ref, back1_ref, back2_ref, back3_ref)
    for block, back_ref in zip(neighbour_blocks()[0], backs):
        back[block_at(block, back_ref.shape[0])] = back_ref[...]
    rows = pick_rows(id_row(halo_ids_ref), 0, acc_ref.shape[0])
    acc = acc_ref[...] + dot(rows, back[...])
    out_ref[...] = acc.astype(BF)
    total = jnp.sum(parts_ref[...].astype(F32).reshape(-1, 8, LANES), axis=0)
    row = lax.broadcasted_iota(jnp.int32, (16, D), 0)
    lead = acc[:16]
    for node in range(COARSE_DEV):
        quarters = [total[4 * node + q : 4 * node + q + 1] for q in range(4)]
        lead += jnp.where(row == node, jnp.concatenate(quarters, axis=1), 0.0)
    out_ref[:16] = lead.astype(BF)


def call(body, outs, args, scratch=(), flops=0, specs=None, out_specs=None, limit=VMEM_LIMIT):
    shapes = [jax.ShapeDtypeStruct(shape, dtype) for shape, dtype in outs]
    moved = sum(a.size * a.dtype.itemsize for a in args)
    moved += sum(s.size * s.dtype.itemsize for s in shapes)
    specs, out_specs = specs or {}, out_specs or {}
    return pl.pallas_call(
        body,
        out_shape=shapes,
        in_specs=[specs.get(i, VMEM) for i in range(len(args))],
        out_specs=[out_specs.get(i, VMEM) for i in range(len(outs))],
        scratch_shapes=list(scratch),
        compiler_params=pltpu.CompilerParams(vmem_limit_bytes=limit),
        cost_estimate=pl.CostEstimate(flops=flops, bytes_accessed=moved, transcendentals=0),
    )(*args)


def trade(blocks):
    count = lax.axis_size(AXES)
    arrived = []
    for block, (step, forward) in zip(blocks, ((PATCH_COLS, 0), (PATCH_COLS, 1), (1, 0), (1, 1))):
        pairs = [
            (p, (p + (step if p // step % 2 != forward else -step)) % count) for p in range(count)
        ]
        arrived.append(lax.ppermute(block, AXES, pairs))
    return arrived


def other_core(value):
    return lax.ppermute(value, "core", [(0, 1), (1, 0)])


def exchange(value):
    chips = lax.axis_size(CHIP)
    blocks = value.reshape(chips, 8, LANES)
    return lax.all_to_all(blocks, CHIP, 0, 0, tiled=True).reshape(chips * 8, LANES)


def shards(
    node_feats,
    edge_feats,
    senders,
    receivers,
    halo_send,
    edge_first,
    edge_second,
    edge_gain,
    node_first,
    node_second,
    node_gain,
    node_cotangent,
    edge_cotangent,
):
    nodes, edges = node_feats.shape[0], edge_feats.shape[0]
    size, blocks = nodes // 4, edges // BLOCK
    devices, chips = lax.axis_size(AXES), lax.axis_size(CHIP)
    coarse_rows = COARSE_DEV * devices
    send, recv = senders.reshape(-1, LANES), receivers.reshape(-1, LANES)
    halo_ids = halo_send.reshape(-1, LANES)
    gain, node_gain = edge_gain[None], node_gain[None]

    spread, *picked = call(
        prepare_kernel,
        [((chips * 8, LANES), BF)] + [((size, D), BF)] * 4,
        (halo_ids, node_feats),
        [pltpu.VMEM((nodes, D), BF)],
        flops=2 * nodes * nodes * D,
    )
    coarse = exchange(spread)
    halos = trade(picked)
    (partial,) = call(
        partial_kernel,
        [((edges, D), F32)],
        (send, recv, edge_feats, node_feats, edge_first),
        [
            pltpu.VMEM((edges, D), BF),
            pltpu.VMEM((nodes, D), BF),
            pltpu.VMEM((3 * D, D), BF),
            pltpu.VMEM((edges, D), F32),
            pltpu.VMEM((2 * nodes, D), BF),
            pltpu.SemaphoreType.DMA((4,)),
            pltpu.SemaphoreType.DMA((edges // STREAM,)),
            pltpu.SemaphoreType.DMA((edges // STREAM, PARTS)),
        ],
        flops=2 * edges * D * (D + 2 * nodes),
        specs={2: ANY, 3: ANY, 4: ANY},
        out_specs={0: ANY},
    )
    coarse, partial, *halos = lax.optimization_barrier((coarse, partial, *halos))
    coarse_other = other_core(coarse)
    edge_out, hidden_bar, node_out, keep, away, node_acc, *grads = call(
        main_kernel,
        [
            ((edges, D), BF),
            ((edges, D), BF),
            ((nodes, D), BF),
            ((chips * 8, LANES), BF),
            ((chips * 8, LANES), BF),
            ((nodes, D), F32),
        ]
        + [((size, D), BF)] * 4,
        (
            send,
            recv,
            gain,
            node_gain,
            partial,
            edge_feats,
            edge_cotangent,
            node_feats,
            node_cotangent,
            *halos,
            coarse,
            coarse_other,
            edge_first,
            edge_second,
            node_first,
            node_second,
        ),
        [
            pltpu.VMEM((edges, D), F32),
            pltpu.VMEM((edges, D), BF),
            pltpu.VMEM((edges, D), BF),
            pltpu.VMEM((nodes, D), BF),
            pltpu.VMEM((nodes, D), BF),
            pltpu.VMEM((nodes, D), BF),
            pltpu.VMEM((2 * chips * 8, LANES), BF),
            pltpu.VMEM((2 * D, D), BF),
            pltpu.VMEM((D, D), BF),
            pltpu.VMEM((2 * D, D), BF),
            pltpu.VMEM((D, D), BF),
            pltpu.VMEM((edges, D), BF),
            pltpu.VMEM((edges, D), BF),
            pltpu.VMEM((nodes + coarse_rows, D), BF),
            pltpu.VMEM((2 * chips * 8, LANES), F32),
            pltpu.VMEM((edges, D), F32),
            pltpu.VMEM((edges, 1), F32),
            pltpu.VMEM((nodes, D), F32),
            pltpu.SemaphoreType.DMA((5, blocks)),
            pltpu.SemaphoreType.DMA((13,)),
        ],
        flops=2 * edges * D * (2 * coarse_rows + 5 * nodes + 2 * D),
        specs={i: ANY for i in range(4, 19)},
        out_specs={0: ANY, 1: ANY},
    )
    (edge_grads,) = call(
        edge_grads_kernel,
        [((edges, D), BF)],
        (hidden_bar, edge_cotangent, edge_first),
        [
            pltpu.VMEM((edges, D), BF),
            pltpu.VMEM((edges, D), BF),
            pltpu.VMEM((D, D), BF),
            pltpu.VMEM((edges, D), BF),
            pltpu.SemaphoreType.DMA((1,)),
            pltpu.SemaphoreType.DMA((edges // STREAM, 2)),
            pltpu.SemaphoreType.DMA((edges // STREAM, PARTS)),
        ],
        flops=2 * edges * D * D,
        specs={0: ANY, 1: ANY, 2: ANY},
        out_specs={0: ANY},
    )
    backs = trade(grads)
    pair = (keep.astype(F32) + other_core(away).astype(F32)).astype(BF)
    parts = exchange(pair)
    parts, *backs = lax.optimization_barrier((parts, *backs))
    (node_grads,) = call(
        final_kernel,
        [((nodes, D), BF)],
        (halo_ids, node_acc, *backs, parts),
        [pltpu.VMEM((nodes, D), BF)],
        limit=FINAL_LIMIT,
        flops=2 * nodes * nodes * D,
    )
    return node_out, edge_out, node_grads, edge_grads


def solution(mesh):
    split = mesh.devices.reshape(-1) if mesh.devices.size != 256 else mesh.devices
    shape = (4, 4, 8, 2) if mesh.devices.size == 256 else (1, 1, 1, mesh.devices.size)
    torus = Mesh(split.reshape(shape), AXES)
    rows, vector, whole = P(AXES, None), P(AXES), P()
    in_specs = (rows, rows, vector, vector, vector) + (whole,) * 6 + (rows, rows)
    return jax.shard_map(
        shards, mesh=torus, in_specs=in_specs, out_specs=(rows,) * 4, check_vma=False
    )
```

```python
import functools

import jax
import jax.numpy as jnp
from jax import lax
from jax.experimental import pallas as pl
from jax.experimental.pallas import tpu as pltpu
from jax.sharding import Mesh
from jax.sharding import PartitionSpec as P

D = 512
COARSE_DEV = 2
PATCH_COLS = 8
LANES = 128
BLOCK = 768
STREAM = 512
PARTS = 2
VMEM_LIMIT = 56 * 1024 * 1024
FINAL_LIMIT = 8 * 1024 * 1024
CHIP = ("x", "y", "z")
AXES = CHIP + ("core",)
BF = jnp.bfloat16
F32 = jnp.float32

VMEM = pl.BlockSpec(memory_space=pltpu.VMEM)
ANY = pl.BlockSpec(memory_space=pl.ANY)


def dot(a, b):
    return jnp.dot(a, b, preferred_element_type=F32)


def dot_nt(a, b):
    return lax.dot_general(a, b, (((1,), (1,)), ((), ())), preferred_element_type=F32)


def dot_tn(a, b):
    return lax.dot_general(a, b, (((0,), (0,)), ((), ())), preferred_element_type=F32)


def pick_rows(ids_row, first, count):
    shape = (count, ids_row.shape[1])
    rows = lax.broadcasted_iota(jnp.int32, shape, 0) + first
    return jnp.where(jnp.broadcast_to(ids_row, shape) == rows, 1.0, 0.0).astype(BF)


def pick_columns(ids_row, first, count):
    size = ids_row.shape[1]
    column = jnp.transpose(jnp.broadcast_to(ids_row, (LANES, size)))
    lane = lax.broadcasted_iota(jnp.int32, (size, LANES), 1) + first
    parts = [
        jnp.where(column == lane + start, 1.0, 0.0).astype(BF) for start in range(0, count, LANES)
    ]
    return jnp.concatenate(parts, axis=1) if len(parts) > 1 else parts[0]


def row_mean(value):
    return jnp.sum(value, axis=-1, keepdims=True) * (1.0 / value.shape[-1])


def normalize(second):
    centred = second - row_mean(second)
    inv_std = lax.rsqrt(row_mean(centred * centred) + 1e-05)
    return centred * inv_std, inv_std


def activate(hidden):
    sigmoid_val = jax.nn.sigmoid(hidden)
    return hidden * sigmoid_val, sigmoid_val * (1.0 + hidden * (1.0 - sigmoid_val))


def normalize_backward(grad_out, gain, normed, inv_std):
    grad_normed = grad_out * gain
    return (
        grad_normed - row_mean(grad_normed) - normed * row_mean(grad_normed * normed)
    ) * inv_std


def block_rows(step):
    return pl.ds(pl.multiple_of(step * BLOCK, BLOCK), BLOCK)


def id_row(ref, first=0, count=None):
    count = ref.shape[0] if count is None else count
    return jnp.concatenate([ref[pl.ds(first + i, 1), :] for i in range(count)], axis=1)


def block_ids(ref, step):
    return id_row(ref, step * (BLOCK // LANES), BLOCK // LANES)


def place_coarse(ids, nodes, coarse_rows):
    devices = coarse_rows // COARSE_DEV
    coarse = ids - 2 * nodes
    node, owner = jnp.bitwise_and(coarse, 1), jnp.right_shift(coarse, 1)
    core = jnp.bitwise_xor(jnp.bitwise_and(owner, 1), lax.axis_index("core"))
    place = node * devices + core * (devices // 2) + jnp.right_shift(owner, 1)
    return jnp.where(coarse < 0, ids, 2 * nodes + place)


def neighbour_blocks():
    index = lax.axis_index("x")
    for axis in AXES[1:]:
        index = index * lax.axis_size(axis) + lax.axis_index(axis)
    core = jnp.bitwise_and(index, 1)
    row = jnp.bitwise_and(index // PATCH_COLS, 1)
    return (3 - row, 2 + row, 1 - core, core), (2 + row, 3 - row, core, 1 - core)


def block_at(block, size):
    return pl.ds(pl.multiple_of(block * size, size), size)


def prepare_kernel(halo_ref, node_ref, spread_ref, out0_ref, out1_ref, out2_ref, out3_ref, picked):
    size = out0_ref.shape[0]
    rows = pick_rows(id_row(halo_ref), 0, node_ref.shape[0])
    picked[...] = dot_tn(rows, node_ref[...]).astype(BF)
    for block, out_ref in zip(neighbour_blocks()[0], (out0_ref, out1_ref, out2_ref, out3_ref)):
        out_ref[...] = picked[block_at(block, size)]
    lead = node_ref[:16].astype(F32)
    quarters = [
        lead[node : node + 1, q * LANES : (q + 1) * LANES]
        for node in range(COARSE_DEV)
        for q in range(4)
    ]
    tile = jnp.concatenate(quarters, axis=0)
    copies = spread_ref.shape[0] // 8
    spread = jnp.broadcast_to(tile[None], (copies, 8, LANES))
    spread_ref[...] = spread.reshape(spread_ref.shape).astype(BF)


def stream_rows(step, part=0, parts=1):
    size = STREAM // parts
    return pl.ds(step * STREAM + part * size, size)


def partial_kernel(
    send_ref,
    recv_ref,
    edge_hbm,
    node_hbm,
    first_hbm,
    out_hbm,
    edge,
    node_ref,
    first,
    out,
    proj,
    sems,
    edge_sems,
    out_sems,
):
    nodes, blocks = node_ref.shape[0], edge.shape[0] // STREAM
    first_copies = [
        pltpu.make_async_copy(
            first_hbm.at[pl.ds(k * D, D), :], first.at[pl.ds(k * D, D), :], sems.at[k]
        )
        for k in range(3)
    ]
    node_copy = pltpu.make_async_copy(node_hbm, node_ref, sems.at[3])
    edge_copies = [
        pltpu.make_async_copy(
            edge_hbm.at[stream_rows(b), :], edge.at[stream_rows(b), :], edge_sems.at[b]
        )
        for b in range(blocks)
    ]
    out_copies = [
        pltpu.make_async_copy(
            out.at[stream_rows(b, p, PARTS), :],
            out_hbm.at[stream_rows(b, p, PARTS), :],
            out_sems.at[b, p],
        )
        for b in range(blocks)
        for p in range(PARTS)
    ]
    first_copies[0].start()
    edge_copies[0].start()
    node_copy.start()
    for k in (1, 2):
        first_copies[k].start()
    for copy in edge_copies[1:]:
        copy.start()
    first_copies[0].wait()
    edge_copies[0].wait()
    out[stream_rows(0), :] = dot(edge[stream_rows(0), :], first[:D])
    node_copy.wait()
    first_copies[1].wait()
    proj[:nodes] = dot(node_ref[...], first[D : 2 * D]).astype(BF)
    first_copies[2].wait()
    proj[nodes:] = dot(node_ref[...], first[2 * D :]).astype(BF)
    groups = STREAM // LANES
    for b in range(blocks):
        rows = stream_rows(b)
        picks = jnp.concatenate(
            [
                pick_columns(id_row(send_ref, b * groups, groups), 0, nodes),
                pick_columns(id_row(recv_ref, b * groups, groups), 0, nodes),
            ],
            axis=1,
        )
        if b == 0:
            out[rows, :] += dot(picks, proj[...])
        else:
            edge_copies[b].wait()
            out[rows, :] = dot(edge[rows, :], first[:D]) + dot(picks, proj[...])
        for copy in out_copies[b * PARTS : (b + 1) * PARTS]:
            copy.start()
    for copy in out_copies:
        copy.wait()


def main_kernel(
    send_ref,
    recv_ref,
    gain_ref,
    node_gain_ref,
    partial_hbm,
    edge_hbm,
    cot_hbm,
    node_hbm,
    node_cot_hbm,
    halo0_hbm,
    halo1_hbm,
    halo2_hbm,
    halo3_hbm,
    coarse0_hbm,
    coarse1_hbm,
    first_hbm,
    second_hbm,
    node_first_hbm,
    node_second_hbm,
    edge_out_hbm,
    hidden_bar_hbm,
    node_out_hbm,
    keep_hbm,
    away_hbm,
    node_acc_hbm,
    grad0_hbm,
    grad1_hbm,
    grad2_hbm,
    grad3_hbm,
    carry,
    edge,
    cot,
    node_ref,
    node_cot_ref,
    halo,
    coarse,
    first,
    second_ref,
    node_first_ref,
    node_second_ref,
    edge_out,
    hidden_bar,
    proj,
    stage,
    normed_all,
    inv_all,
    summed_all,
    node_out,
    keep,
    away,
    node_acc_all,
    block_sems,
    sems,
    out_sems,
):
    blocks, nodes = cot.shape[0] // BLOCK, node_ref.shape[0]
    table = proj.shape[0]
    coarse_rows = table - nodes
    size = nodes // 4
    received_blocks = neighbour_blocks()[1]
    half = coarse.shape[0] // 2
    parity = coarse_rows // COARSE_DEV

    halo_copies = [
        pltpu.make_async_copy(source, halo.at[block_at(block, size), :], sems.at[k])
        for k, (block, source) in enumerate(
            zip(received_blocks, (halo0_hbm, halo1_hbm, halo2_hbm, halo3_hbm))
        )
    ]
    coarse_copies = [
        pltpu.make_async_copy(source, coarse.at[pl.ds(k * half, half), :], sems.at[4 + k])
        for k, source in enumerate((coarse0_hbm, coarse1_hbm))
    ]
    first_copy, last_copy = [
        pltpu.make_async_copy(
            first_hbm.at[pl.ds((k + 1) * D, D), :], first.at[pl.ds(k * D, D), :], sems.at[slot]
        )
        for k, slot in ((0, 6), (1, 12))
    ]
    second_copy = pltpu.make_async_copy(second_hbm, second_ref, sems.at[7])
    node_copies = [
        pltpu.make_async_copy(source, target, sems.at[8 + k])
        for k, (source, target) in enumerate(
            (
                (node_hbm, node_ref),
                (node_first_hbm, node_first_ref),
                (node_second_hbm, node_second_ref),
                (node_cot_hbm, node_cot_ref),
            )
        )
    ]

    node_out_copy, keep_copy, away_copy, node_acc_copy = [
        pltpu.make_async_copy(source, target, out_sems.at[k])
        for k, (source, target) in enumerate(
            (
                (node_out, node_out_hbm),
                (keep, keep_hbm),
                (away, away_hbm),
                (node_acc_all, node_acc_hbm),
            )
        )
    ]
    grad_copies = [
        pltpu.make_async_copy(halo.at[block_at(block, size), :], target, out_sems.at[4 + k])
        for k, (block, target) in enumerate(
            zip(received_blocks, (grad0_hbm, grad1_hbm, grad2_hbm, grad3_hbm))
        )
    ]

    def fetch(source, target, slot, step):
        rows = block_rows(step)
        return pltpu.make_async_copy(
            source.at[rows, :], target.at[rows, :], block_sems.at[slot, step]
        )

    edge_copy = functools.partial(fetch, edge_hbm, edge, 0)
    cot_copy = functools.partial(fetch, cot_hbm, cot, 1)
    edge_out_copy = functools.partial(fetch, edge_out, edge_out_hbm, 2)
    hidden_bar_copy = functools.partial(fetch, hidden_bar, hidden_bar_hbm, 3)
    carry_copy = functools.partial(fetch, partial_hbm, carry, 4)

    first_copy.start()
    for copy in halo_copies + coarse_copies:
        copy.start()
    carry_copy(0).start()
    second_copy.start()
    edge_copy(0).start()
    for step in range(1, blocks):
        carry_copy(step).start()
        edge_copy(step).start()
    for copy in node_copies:
        copy.start()
    for step in range(blocks):
        cot_copy(step).start()
    last_copy.start()

    first_copy.wait()
    for copy in halo_copies:
        copy.wait()
    proj[:nodes] = dot(halo[...], first[:D]).astype(BF)
    for copy in coarse_copies:
        copy.wait()
    stage[...] = coarse[...].astype(F32)
    for row in range(COARSE_DEV):
        latents = jnp.concatenate(
            [stage[pl.ds(4 * row + column, parity, 8), :] for column in range(4)], axis=1
        )
        start = nodes + row * parity
        proj[start : start + parity] = dot(latents.astype(BF), first[:D]).astype(BF)
    summed_all[...] = jnp.zeros_like(summed_all)
    second_copy.wait()

    @pl.loop(0, blocks, unroll=True)
    def _(step):
        rows = block_rows(step)
        ids = place_coarse(block_ids(send_ref, step), nodes, coarse_rows)
        picks = pick_columns(ids, nodes, table)
        normed_all[rows, :] = dot(picks, proj[...])
        carry_copy(step).wait()
        hidden = carry[rows, :] + normed_all[rows, :]
        active, carry[rows, :] = activate(hidden)
        normed, inv_std = normalize(dot(active.astype(BF), second_ref[...]))
        normed_all[rows, :] = normed
        inv_all[rows, :] = inv_std
        message = normed * gain_ref[...]
        summed_all[...] += dot(
            pick_rows(block_ids(recv_ref, step), 0, nodes), message.astype(BF)
        )
        edge_copy(step).wait()
        edge_out[rows, :] = (edge[rows, :].astype(F32) + message).astype(BF)
        edge_out_copy(step).start()

    for copy in node_copies:
        copy.wait()
    summed = summed_all[...].astype(BF)
    node_feats = node_ref[...]
    hidden = dot(node_feats, node_first_ref[:D]) + dot(summed, node_first_ref[D:])
    active, node_slope = activate(hidden)
    normed, inv_std = normalize(dot(active.astype(BF), node_second_ref[...]))
    node_out[...] = (node_feats.astype(F32) + normed * node_gain_ref[...]).astype(BF)
    node_out_copy.start()
    node_bar = node_cot_ref[...].astype(F32)
    second_bar = normalize_backward(node_bar, node_gain_ref[...], normed, inv_std)
    active_bar = dot_nt(second_bar.astype(BF), node_second_ref[...])
    node_hidden_bar = (active_bar * node_slope).astype(BF)
    node_acc = node_bar + dot_nt(node_hidden_bar, node_first_ref[:D])
    summed_bar = dot_nt(node_hidden_bar, node_first_ref[D:]).astype(BF)

    @pl.loop(0, blocks, unroll=True)
    def _(step):
        rows = block_rows(step)
        cot_copy(step).wait()
        picks = pick_columns(block_ids(recv_ref, step), 0, nodes)
        message_bar = cot[rows, :].astype(F32) + dot(picks, summed_bar)
        second_bar = normalize_backward(
            message_bar, gain_ref[...], normed_all[rows, :], inv_all[rows, :]
        )
        active_bar = dot_nt(second_bar.astype(BF), second_ref[...])
        hidden_bar[rows, :] = (active_bar * carry[rows, :]).astype(BF)
        hidden_bar_copy(step).start()

    send = place_coarse(id_row(send_ref), nodes, coarse_rows)

    def sender_grads(start, count):
        sums = dot(pick_rows(send, start, count), hidden_bar[...])
        return dot_nt(sums.astype(BF), first[:D])

    last_copy.wait()
    received = dot(pick_rows(id_row(recv_ref), 0, nodes), hidden_bar[...])
    node_acc += sender_grads(0, nodes) + dot_nt(received.astype(BF), first[D:])
    node_acc_all[...] = node_acc
    node_acc_copy.start()
    for row in range(COARSE_DEV):
        grads = sender_grads(2 * nodes + row * parity, parity)
        for column in range(4):
            stage[pl.ds(4 * row + column, parity, 8), :] = grads[
                :, column * LANES : (column + 1) * LANES
            ]
    keep[...] = stage[:half].astype(BF)
    keep_copy.start()
    away[...] = stage[half:].astype(BF)
    away_copy.start()
    halo[...] = sender_grads(nodes, nodes).astype(BF)
    for copy in grad_copies:
        copy.start()
    for step in range(blocks):
        edge_out_copy(step).wait()
        hidden_bar_copy(step).wait()
    for copy in [node_out_copy, keep_copy, away_copy, node_acc_copy] + grad_copies:
        copy.wait()


def edge_grads_kernel(
    hidden_bar_hbm, cot_hbm, first_hbm, out_hbm, hidden_bar, cot, first, out, sem, in_sems, out_sems
):
    blocks = out.shape[0] // STREAM
    first_copy = pltpu.make_async_copy(first_hbm.at[pl.ds(0, D), :], first, sem.at[0])
    in_copies = [
        [
            pltpu.make_async_copy(
                source.at[stream_rows(b), :], target.at[stream_rows(b), :], in_sems.at[b, k]
            )
            for k, (source, target) in enumerate(((hidden_bar_hbm, hidden_bar), (cot_hbm, cot)))
        ]
        for b in range(blocks)
    ]
    out_copies = [
        pltpu.make_async_copy(
            out.at[stream_rows(b, p, PARTS), :],
            out_hbm.at[stream_rows(b, p, PARTS), :],
            out_sems.at[b, p],
        )
        for b in range(blocks)
        for p in range(PARTS)
    ]
    first_copy.start()
    for pair in in_copies:
        for copy in pair:
            copy.start()
    first_copy.wait()
    for b in range(blocks):
        rows = stream_rows(b)
        for copy in in_copies[b]:
            copy.wait()
        grad = dot_nt(hidden_bar[rows, :], first[...])
        out[rows, :] = (cot[rows, :].astype(F32) + grad).astype(BF)
        for copy in out_copies[b * PARTS : (b + 1) * PARTS]:
            copy.start()
    for copy in out_copies:
        copy.wait()


def final_kernel(
    halo_ids_ref, acc_ref, back0_ref, back1_ref, back2_ref, back3_ref, parts_ref, out_ref, back
):
    backs = (back0_ref, back1_ref, back2_ref, back3_ref)
    for block, back_ref in zip(neighbour_blocks()[0], backs):
        back[block_at(block, back_ref.shape[0])] = back_ref[...]
    rows = pick_rows(id_row(halo_ids_ref), 0, acc_ref.shape[0])
    acc = acc_ref[...] + dot(rows, back[...])
    out_ref[...] = acc.astype(BF)
    total = jnp.sum(parts_ref[...].astype(F32).reshape(-1, 8, LANES), axis=0)
    row = lax.broadcasted_iota(jnp.int32, (16, D), 0)
    lead = acc[:16]
    for node in range(COARSE_DEV):
        quarters = [total[4 * node + q : 4 * node + q + 1] for q in range(4)]
        lead += jnp.where(row == node, jnp.concatenate(quarters, axis=1), 0.0)
    out_ref[:16] = lead.astype(BF)


def call(body, outs, args, scratch=(), flops=0, specs=None, out_specs=None, limit=VMEM_LIMIT):
    shapes = [jax.ShapeDtypeStruct(shape, dtype) for shape, dtype in outs]
    moved = sum(a.size * a.dtype.itemsize for a in args)
    moved += sum(s.size * s.dtype.itemsize for s in shapes)
    specs, out_specs = specs or {}, out_specs or {}
    return pl.pallas_call(
        body,
        out_shape=shapes,
        in_specs=[specs.get(i, VMEM) for i in range(len(args))],
        out_specs=[out_specs.get(i, VMEM) for i in range(len(outs))],
        scratch_shapes=list(scratch),
        compiler_params=pltpu.CompilerParams(vmem_limit_bytes=limit),
        cost_estimate=pl.CostEstimate(flops=flops, bytes_accessed=moved, transcendentals=0),
    )(*args)


def trade(blocks):
    count = lax.axis_size(AXES)
    arrived = []
    for block, (step, forward) in zip(blocks, ((PATCH_COLS, 0), (PATCH_COLS, 1), (1, 0), (1, 1))):
        pairs = [
            (p, (p + (step if p // step % 2 != forward else -step)) % count) for p in range(count)
        ]
        arrived.append(lax.ppermute(block, AXES, pairs))
    return arrived


def other_core(value):
    return lax.ppermute(value, "core", [(0, 1), (1, 0)])


def exchange(value):
    chips = lax.axis_size(CHIP)
    blocks = value.reshape(chips, 8, LANES)
    return lax.all_to_all(blocks, CHIP, 0, 0, tiled=True).reshape(chips * 8, LANES)


def shards(
    node_feats,
    edge_feats,
    senders,
    receivers,
    halo_send,
    edge_first,
    edge_second,
    edge_gain,
    node_first,
    node_second,
    node_gain,
    node_cotangent,
    edge_cotangent,
):
    nodes, edges = node_feats.shape[0], edge_feats.shape[0]
    size, blocks = nodes // 4, edges // BLOCK
    devices, chips = lax.axis_size(AXES), lax.axis_size(CHIP)
    coarse_rows = COARSE_DEV * devices
    send, recv = senders.reshape(-1, LANES), receivers.reshape(-1, LANES)
    halo_ids = halo_send.reshape(-1, LANES)
    gain, node_gain = edge_gain[None], node_gain[None]

    spread, *picked = call(
        prepare_kernel,
        [((chips * 8, LANES), BF)] + [((size, D), BF)] * 4,
        (halo_ids, node_feats),
        [pltpu.VMEM((nodes, D), BF)],
        flops=2 * nodes * nodes * D,
    )
    coarse = exchange(spread)
    halos = trade(picked)
    (partial,) = call(
        partial_kernel,
        [((edges, D), F32)],
        (send, recv, edge_feats, node_feats, edge_first),
        [
            pltpu.VMEM((edges, D), BF),
            pltpu.VMEM((nodes, D), BF),
            pltpu.VMEM((3 * D, D), BF),
            pltpu.VMEM((edges, D), F32),
            pltpu.VMEM((2 * nodes, D), BF),
            pltpu.SemaphoreType.DMA((4,)),
            pltpu.SemaphoreType.DMA((edges // STREAM,)),
            pltpu.SemaphoreType.DMA((edges // STREAM, PARTS)),
        ],
        flops=2 * edges * D * (D + 2 * nodes),
        specs={2: ANY, 3: ANY, 4: ANY},
        out_specs={0: ANY},
    )
    coarse, partial, *halos = lax.optimization_barrier((coarse, partial, *halos))
    coarse_other = other_core(coarse)
    edge_out, hidden_bar, node_out, keep, away, node_acc, *grads = call(
        main_kernel,
        [
            ((edges, D), BF),
            ((edges, D), BF),
            ((nodes, D), BF),
            ((chips * 8, LANES), BF),
            ((chips * 8, LANES), BF),
            ((nodes, D), F32),
        ]
        + [((size, D), BF)] * 4,
        (
            send,
            recv,
            gain,
            node_gain,
            partial,
            edge_feats,
            edge_cotangent,
            node_feats,
            node_cotangent,
            *halos,
            coarse,
            coarse_other,
            edge_first,
            edge_second,
            node_first,
            node_second,
        ),
        [
            pltpu.VMEM((edges, D), F32),
            pltpu.VMEM((edges, D), BF),
            pltpu.VMEM((edges, D), BF),
            pltpu.VMEM((nodes, D), BF),
            pltpu.VMEM((nodes, D), BF),
            pltpu.VMEM((nodes, D), BF),
            pltpu.VMEM((2 * chips * 8, LANES), BF),
            pltpu.VMEM((2 * D, D), BF),
            pltpu.VMEM((D, D), BF),
            pltpu.VMEM((2 * D, D), BF),
            pltpu.VMEM((D, D), BF),
            pltpu.VMEM((edges, D), BF),
            pltpu.VMEM((edges, D), BF),
            pltpu.VMEM((nodes + coarse_rows, D), BF),
            pltpu.VMEM((2 * chips * 8, LANES), F32),
            pltpu.VMEM((edges, D), F32),
            pltpu.VMEM((edges, 1), F32),
            pltpu.VMEM((nodes, D), F32),
            pltpu.VMEM((nodes, D), BF),
            pltpu.VMEM((chips * 8, LANES), BF),
            pltpu.VMEM((chips * 8, LANES), BF),
            pltpu.VMEM((nodes, D), F32),
            pltpu.SemaphoreType.DMA((5, blocks)),
            pltpu.SemaphoreType.DMA((13,)),
            pltpu.SemaphoreType.DMA((8,)),
        ],
        flops=2 * edges * D * (2 * coarse_rows + 5 * nodes + 2 * D),
        specs={i: ANY for i in range(4, 19)},
        out_specs={i: ANY for i in range(10)},
    )
    (edge_grads,) = call(
        edge_grads_kernel,
        [((edges, D), BF)],
        (hidden_bar, edge_cotangent, edge_first),
        [
            pltpu.VMEM((edges, D), BF),
            pltpu.VMEM((edges, D), BF),
            pltpu.VMEM((D, D), BF),
            pltpu.VMEM((edges, D), BF),
            pltpu.SemaphoreType.DMA((1,)),
            pltpu.SemaphoreType.DMA((edges // STREAM, 2)),
            pltpu.SemaphoreType.DMA((edges // STREAM, PARTS)),
        ],
        flops=2 * edges * D * D,
        specs={0: ANY, 1: ANY, 2: ANY},
        out_specs={0: ANY},
    )
    backs = trade(grads)
    pair = (keep.astype(F32) + other_core(away).astype(F32)).astype(BF)
    parts = exchange(pair)
    parts, *backs = lax.optimization_barrier((parts, *backs))
    (node_grads,) = call(
        final_kernel,
        [((nodes, D), BF)],
        (halo_ids, node_acc, *backs, parts),
        [pltpu.VMEM((nodes, D), BF)],
        limit=FINAL_LIMIT,
        flops=2 * nodes * nodes * D,
    )
    return node_out, edge_out, node_grads, edge_grads


def solution(mesh):
    split = mesh.devices.reshape(-1) if mesh.devices.size != 256 else mesh.devices
    shape = (4, 4, 8, 2) if mesh.devices.size == 256 else (1, 1, 1, mesh.devices.size)
    torus = Mesh(split.reshape(shape), AXES)
    rows, vector, whole = P(AXES, None), P(AXES), P()
    in_specs = (rows, rows, vector, vector, vector) + (whole,) * 6 + (rows, rows)
    return jax.shard_map(
        shards, mesh=torus, in_specs=in_specs, out_specs=(rows,) * 4, check_vma=False
    )
```

```python
import functools

import jax
import jax.numpy as jnp
from jax import lax
from jax.experimental import pallas as pl
from jax.experimental.pallas import tpu as pltpu
from jax.sharding import Mesh
from jax.sharding import PartitionSpec as P

D = 512
COARSE_DEV = 2
PATCH_COLS = 8
LANES = 128
BLOCK = 768
STREAM = 512
PARTS = 2
VMEM_LIMIT = 56 * 1024 * 1024
FINAL_LIMIT = 8 * 1024 * 1024
CHIP = ("x", "y", "z")
AXES = CHIP + ("core",)
BF = jnp.bfloat16
F32 = jnp.float32

VMEM = pl.BlockSpec(memory_space=pltpu.VMEM)
ANY = pl.BlockSpec(memory_space=pl.ANY)


def dot(a, b):
    return jnp.dot(a, b, preferred_element_type=F32)


def dot_nt(a, b):
    return lax.dot_general(a, b, (((1,), (1,)), ((), ())), preferred_element_type=F32)


def dot_tn(a, b):
    return lax.dot_general(a, b, (((0,), (0,)), ((), ())), preferred_element_type=F32)


def pick_rows(ids_row, first, count):
    shape = (count, ids_row.shape[1])
    rows = lax.broadcasted_iota(jnp.int32, shape, 0) + first
    return jnp.where(jnp.broadcast_to(ids_row, shape) == rows, 1.0, 0.0).astype(BF)


def pick_columns(ids_row, first, count):
    size = ids_row.shape[1]
    column = jnp.transpose(jnp.broadcast_to(ids_row, (LANES, size)))
    lane = lax.broadcasted_iota(jnp.int32, (size, LANES), 1) + first
    parts = [
        jnp.where(column == lane + start, 1.0, 0.0).astype(BF) for start in range(0, count, LANES)
    ]
    return jnp.concatenate(parts, axis=1) if len(parts) > 1 else parts[0]


def row_mean(value):
    return jnp.sum(value, axis=-1, keepdims=True) * (1.0 / value.shape[-1])


def normalize(second):
    centred = second - row_mean(second)
    inv_std = lax.rsqrt(row_mean(centred * centred) + 1e-05)
    return centred * inv_std, inv_std


def activate(hidden):
    sigmoid_val = jax.nn.sigmoid(hidden)
    return hidden * sigmoid_val, sigmoid_val * (1.0 + hidden * (1.0 - sigmoid_val))


def normalize_backward(grad_out, gain, normed, inv_std):
    grad_normed = grad_out * gain
    return (
        grad_normed - row_mean(grad_normed) - normed * row_mean(grad_normed * normed)
    ) * inv_std


def block_rows(step):
    return pl.ds(pl.multiple_of(step * BLOCK, BLOCK), BLOCK)


def id_row(ref, first=0, count=None):
    count = ref.shape[0] if count is None else count
    return jnp.concatenate([ref[pl.ds(first + i, 1), :] for i in range(count)], axis=1)


def block_ids(ref, step):
    return id_row(ref, step * (BLOCK // LANES), BLOCK // LANES)


def place_coarse(ids, nodes, coarse_rows):
    devices = coarse_rows // COARSE_DEV
    coarse = ids - 2 * nodes
    node, owner = jnp.bitwise_and(coarse, 1), jnp.right_shift(coarse, 1)
    core = jnp.bitwise_xor(jnp.bitwise_and(owner, 1), lax.axis_index("core"))
    place = node * devices + core * (devices // 2) + jnp.right_shift(owner, 1)
    return jnp.where(coarse < 0, ids, 2 * nodes + place)


def neighbour_blocks():
    index = lax.axis_index("x")
    for axis in AXES[1:]:
        index = index * lax.axis_size(axis) + lax.axis_index(axis)
    core = jnp.bitwise_and(index, 1)
    row = jnp.bitwise_and(index // PATCH_COLS, 1)
    return (3 - row, 2 + row, 1 - core, core), (2 + row, 3 - row, core, 1 - core)


def block_at(block, size):
    return pl.ds(pl.multiple_of(block * size, size), size)


def prepare_kernel(halo_ref, node_ref, spread_ref, out0_ref, out1_ref, out2_ref, out3_ref, picked):
    size = out0_ref.shape[0]
    rows = pick_rows(id_row(halo_ref), 0, node_ref.shape[0])
    picked[...] = dot_tn(rows, node_ref[...]).astype(BF)
    for block, out_ref in zip(neighbour_blocks()[0], (out0_ref, out1_ref, out2_ref, out3_ref)):
        out_ref[...] = picked[block_at(block, size)]
    lead = node_ref[:16].astype(F32)
    quarters = [
        lead[node : node + 1, q * LANES : (q + 1) * LANES]
        for node in range(COARSE_DEV)
        for q in range(4)
    ]
    tile = jnp.concatenate(quarters, axis=0)
    copies = spread_ref.shape[0] // 8
    spread = jnp.broadcast_to(tile[None], (copies, 8, LANES))
    spread_ref[...] = spread.reshape(spread_ref.shape).astype(BF)


def stream_rows(step, part=0, parts=1):
    size = STREAM // parts
    return pl.ds(step * STREAM + part * size, size)


def partial_kernel(
    send_ref,
    recv_ref,
    edge_hbm,
    node_hbm,
    first_hbm,
    out_hbm,
    edge,
    node_ref,
    first,
    out,
    proj,
    sems,
    edge_sems,
    out_sems,
):
    nodes, blocks = node_ref.shape[0], edge.shape[0] // STREAM
    first_copies = [
        pltpu.make_async_copy(
            first_hbm.at[pl.ds(k * D, D), :], first.at[pl.ds(k * D, D), :], sems.at[k]
        )
        for k in range(3)
    ]
    node_copy = pltpu.make_async_copy(node_hbm, node_ref, sems.at[3])
    edge_copies = [
        pltpu.make_async_copy(
            edge_hbm.at[stream_rows(b), :], edge.at[stream_rows(b), :], edge_sems.at[b]
        )
        for b in range(blocks)
    ]
    out_copies = [
        pltpu.make_async_copy(
            out.at[stream_rows(b, p, PARTS), :],
            out_hbm.at[stream_rows(b, p, PARTS), :],
            out_sems.at[b, p],
        )
        for b in range(blocks)
        for p in range(PARTS)
    ]
    first_copies[0].start()
    edge_copies[0].start()
    node_copy.start()
    for k in (1, 2):
        first_copies[k].start()
    for copy in edge_copies[1:]:
        copy.start()
    first_copies[0].wait()
    edge_copies[0].wait()
    out[stream_rows(0), :] = dot(edge[stream_rows(0), :], first[:D])
    node_copy.wait()
    first_copies[1].wait()
    proj[:nodes] = dot(node_ref[...], first[D : 2 * D]).astype(BF)
    first_copies[2].wait()
    proj[nodes:] = dot(node_ref[...], first[2 * D :]).astype(BF)
    groups = STREAM // LANES
    for b in range(blocks):
        rows = stream_rows(b)
        picks = jnp.concatenate(
            [
                pick_columns(id_row(send_ref, b * groups, groups), 0, nodes),
                pick_columns(id_row(recv_ref, b * groups, groups), 0, nodes),
            ],
            axis=1,
        )
        if b == 0:
            out[rows, :] += dot(picks, proj[...])
        else:
            edge_copies[b].wait()
            out[rows, :] = dot(edge[rows, :], first[:D]) + dot(picks, proj[...])
        for copy in out_copies[b * PARTS : (b + 1) * PARTS]:
            copy.start()
    for copy in out_copies:
        copy.wait()


def main_kernel(
    send_ref,
    recv_ref,
    gain_ref,
    node_gain_ref,
    partial_hbm,
    edge_hbm,
    cot_hbm,
    node_hbm,
    node_cot_hbm,
    halo0_hbm,
    halo1_hbm,
    halo2_hbm,
    halo3_hbm,
    coarse0_hbm,
    coarse1_hbm,
    first_hbm,
    second_hbm,
    node_first_hbm,
    node_second_hbm,
    edge_out_hbm,
    hidden_bar_hbm,
    node_out_hbm,
    keep_hbm,
    away_hbm,
    node_acc_hbm,
    grad0_hbm,
    grad1_hbm,
    grad2_hbm,
    grad3_hbm,
    carry,
    edge,
    cot,
    node_ref,
    node_cot_ref,
    halo,
    coarse,
    first,
    second_ref,
    node_first_ref,
    node_second_ref,
    edge_out,
    hidden_bar,
    proj,
    stage,
    normed_all,
    inv_all,
    summed_all,
    node_out,
    keep,
    away,
    node_acc_all,
    block_sems,
    sems,
    out_sems,
):
    blocks, nodes = cot.shape[0] // BLOCK, node_ref.shape[0]
    table = proj.shape[0]
    coarse_rows = table - nodes
    size = nodes // 4
    received_blocks = neighbour_blocks()[1]
    half = coarse.shape[0] // 2
    parity = coarse_rows // COARSE_DEV

    halo_copies = [
        pltpu.make_async_copy(source, halo.at[block_at(block, size), :], sems.at[k])
        for k, (block, source) in enumerate(
            zip(received_blocks, (halo0_hbm, halo1_hbm, halo2_hbm, halo3_hbm))
        )
    ]
    coarse_copies = [
        pltpu.make_async_copy(source, coarse.at[pl.ds(k * half, half), :], sems.at[4 + k])
        for k, source in enumerate((coarse0_hbm, coarse1_hbm))
    ]
    first_copy, last_copy = [
        pltpu.make_async_copy(
            first_hbm.at[pl.ds((k + 1) * D, D), :], first.at[pl.ds(k * D, D), :], sems.at[slot]
        )
        for k, slot in ((0, 6), (1, 12))
    ]
    second_copy = pltpu.make_async_copy(second_hbm, second_ref, sems.at[7])
    node_copies = [
        pltpu.make_async_copy(source, target, sems.at[8 + k])
        for k, (source, target) in enumerate(
            (
                (node_hbm, node_ref),
                (node_first_hbm, node_first_ref),
                (node_second_hbm, node_second_ref),
                (node_cot_hbm, node_cot_ref),
            )
        )
    ]

    node_out_copy, keep_copy, away_copy, node_acc_copy = [
        pltpu.make_async_copy(source, target, out_sems.at[k])
        for k, (source, target) in enumerate(
            (
                (node_out, node_out_hbm),
                (keep, keep_hbm),
                (away, away_hbm),
                (node_acc_all, node_acc_hbm),
            )
        )
    ]
    grad_copies = [
        pltpu.make_async_copy(halo.at[block_at(block, size), :], target, out_sems.at[4 + k])
        for k, (block, target) in enumerate(
            zip(received_blocks, (grad0_hbm, grad1_hbm, grad2_hbm, grad3_hbm))
        )
    ]

    def fetch(source, target, slot, step):
        rows = block_rows(step)
        return pltpu.make_async_copy(
            source.at[rows, :], target.at[rows, :], block_sems.at[slot, step]
        )

    edge_copy = functools.partial(fetch, edge_hbm, edge, 0)
    cot_copy = functools.partial(fetch, cot_hbm, cot, 1)
    edge_out_copy = functools.partial(fetch, edge_out, edge_out_hbm, 2)
    hidden_bar_copy = functools.partial(fetch, hidden_bar, hidden_bar_hbm, 3)
    carry_copy = functools.partial(fetch, partial_hbm, carry, 4)

    first_copy.start()
    for copy in halo_copies + coarse_copies:
        copy.start()
    carry_copy(0).start()
    second_copy.start()
    edge_copy(0).start()
    for step in range(1, blocks):
        carry_copy(step).start()
        edge_copy(step).start()
    for copy in node_copies:
        copy.start()
    for step in range(blocks):
        cot_copy(step).start()
    last_copy.start()

    first_copy.wait()
    for copy in halo_copies:
        copy.wait()
    proj[:nodes] = dot(halo[...], first[:D]).astype(BF)
    for copy in coarse_copies:
        copy.wait()
    stage[...] = coarse[...].astype(F32)
    for row in range(COARSE_DEV):
        latents = jnp.concatenate(
            [stage[pl.ds(4 * row + column, parity, 8), :] for column in range(4)], axis=1
        )
        start = nodes + row * parity
        proj[start : start + parity] = dot(latents.astype(BF), first[:D]).astype(BF)
    summed_all[...] = jnp.zeros_like(summed_all)
    second_copy.wait()

    @pl.loop(0, blocks, unroll=True)
    def _(step):
        rows = block_rows(step)
        ids = place_coarse(block_ids(send_ref, step), nodes, coarse_rows)
        picks = pick_columns(ids, nodes, table)
        normed_all[rows, :] = dot(picks, proj[...])
        carry_copy(step).wait()
        hidden = carry[rows, :] + normed_all[rows, :]
        active, carry[rows, :] = activate(hidden)
        normed, inv_std = normalize(dot(active.astype(BF), second_ref[...]))
        normed_all[rows, :] = normed
        inv_all[rows, :] = inv_std
        message = normed * gain_ref[...]
        summed_all[...] += dot(
            pick_rows(block_ids(recv_ref, step), 0, nodes), message.astype(BF)
        )
        edge_copy(step).wait()
        edge_out[rows, :] = (edge[rows, :].astype(F32) + message).astype(BF)
        edge_out_copy(step).start()

    for copy in node_copies:
        copy.wait()
    summed = summed_all[...].astype(BF)
    node_feats = node_ref[...]
    hidden = dot(node_feats, node_first_ref[:D]) + dot(summed, node_first_ref[D:])
    active, node_slope = activate(hidden)
    normed, inv_std = normalize(dot(active.astype(BF), node_second_ref[...]))
    node_out[...] = (node_feats.astype(F32) + normed * node_gain_ref[...]).astype(BF)
    node_out_copy.start()
    node_bar = node_cot_ref[...].astype(F32)
    second_bar = normalize_backward(node_bar, node_gain_ref[...], normed, inv_std)
    active_bar = dot_nt(second_bar.astype(BF), node_second_ref[...])
    node_hidden_bar = (active_bar * node_slope).astype(BF)
    node_acc = node_bar + dot_nt(node_hidden_bar, node_first_ref[:D])
    summed_bar = dot_nt(node_hidden_bar, node_first_ref[D:]).astype(BF)

    @pl.loop(0, blocks, unroll=True)
    def _(step):
        rows = block_rows(step)
        cot_copy(step).wait()
        picks = pick_columns(block_ids(recv_ref, step), 0, nodes)
        message_bar = cot[rows, :].astype(F32) + dot(picks, summed_bar)
        second_bar = normalize_backward(
            message_bar, gain_ref[...], normed_all[rows, :], inv_all[rows, :]
        )
        active_bar = dot_nt(second_bar.astype(BF), second_ref[...])
        hidden_bar[rows, :] = (active_bar * carry[rows, :]).astype(BF)
        hidden_bar_copy(step).start()

    send = place_coarse(id_row(send_ref), nodes, coarse_rows)

    def sender_grads(start, count):
        sums = dot(pick_rows(send, start, count), hidden_bar[...])
        return dot_nt(sums.astype(BF), first[:D])

    last_copy.wait()
    received = dot(pick_rows(id_row(recv_ref), 0, nodes), hidden_bar[...])
    node_acc += sender_grads(0, nodes) + dot_nt(received.astype(BF), first[D:])
    node_acc_all[...] = node_acc
    node_acc_copy.start()
    for row in range(COARSE_DEV):
        grads = sender_grads(2 * nodes + row * parity, parity)
        for column in range(4):
            stage[pl.ds(4 * row + column, parity, 8), :] = grads[
                :, column * LANES : (column + 1) * LANES
            ]
    keep[...] = stage[:half].astype(BF)
    keep_copy.start()
    away[...] = stage[half:].astype(BF)
    away_copy.start()
    halo[...] = sender_grads(nodes, nodes).astype(BF)
    for copy in grad_copies:
        copy.start()
    for step in range(blocks):
        edge_out_copy(step).wait()
        hidden_bar_copy(step).wait()
    for copy in [node_out_copy, keep_copy, away_copy, node_acc_copy] + grad_copies:
        copy.wait()


def edge_grads_kernel(
    hidden_bar_hbm, cot_hbm, first_hbm, out_hbm, hidden_bar, cot, first, out, sem, in_sems, out_sems
):
    blocks = out.shape[0] // STREAM
    first_copy = pltpu.make_async_copy(first_hbm.at[pl.ds(0, D), :], first, sem.at[0])
    in_copies = [
        [
            pltpu.make_async_copy(
                source.at[stream_rows(b), :], target.at[stream_rows(b), :], in_sems.at[b, k]
            )
            for k, (source, target) in enumerate(((hidden_bar_hbm, hidden_bar), (cot_hbm, cot)))
        ]
        for b in range(blocks)
    ]
    out_copies = [
        pltpu.make_async_copy(
            out.at[stream_rows(b, p, PARTS), :],
            out_hbm.at[stream_rows(b, p, PARTS), :],
            out_sems.at[b, p],
        )
        for b in range(blocks)
        for p in range(PARTS)
    ]
    first_copy.start()
    for pair in in_copies:
        for copy in pair:
            copy.start()
    first_copy.wait()
    for b in range(blocks):
        rows = stream_rows(b)
        for copy in in_copies[b]:
            copy.wait()
        grad = dot_nt(hidden_bar[rows, :], first[...])
        out[rows, :] = (cot[rows, :].astype(F32) + grad).astype(BF)
        for copy in out_copies[b * PARTS : (b + 1) * PARTS]:
            copy.start()
    for copy in out_copies:
        copy.wait()


def pair_kernel(keep_ref, arrived_ref, out_ref):
    out_ref[...] = (keep_ref[...].astype(F32) + arrived_ref[...].astype(F32)).astype(BF)


def final_kernel(
    halo_ids_ref, acc_ref, back0_ref, back1_ref, back2_ref, back3_ref, parts_ref, out_ref, back
):
    backs = (back0_ref, back1_ref, back2_ref, back3_ref)
    for block, back_ref in zip(neighbour_blocks()[0], backs):
        back[block_at(block, back_ref.shape[0])] = back_ref[...]
    rows = pick_rows(id_row(halo_ids_ref), 0, acc_ref.shape[0])
    acc = acc_ref[...] + dot(rows, back[...])
    out_ref[...] = acc.astype(BF)
    total = jnp.sum(parts_ref[...].astype(F32).reshape(-1, 8, LANES), axis=0)
    row = lax.broadcasted_iota(jnp.int32, (16, D), 0)
    lead = acc[:16]
    for node in range(COARSE_DEV):
        quarters = [total[4 * node + q : 4 * node + q + 1] for q in range(4)]
        lead += jnp.where(row == node, jnp.concatenate(quarters, axis=1), 0.0)
    out_ref[:16] = lead.astype(BF)


def call(body, outs, args, scratch=(), flops=0, specs=None, out_specs=None, limit=VMEM_LIMIT):
    shapes = [jax.ShapeDtypeStruct(shape, dtype) for shape, dtype in outs]
    moved = sum(a.size * a.dtype.itemsize for a in args)
    moved += sum(s.size * s.dtype.itemsize for s in shapes)
    specs, out_specs = specs or {}, out_specs or {}
    return pl.pallas_call(
        body,
        out_shape=shapes,
        in_specs=[specs.get(i, VMEM) for i in range(len(args))],
        out_specs=[out_specs.get(i, VMEM) for i in range(len(outs))],
        scratch_shapes=list(scratch),
        compiler_params=pltpu.CompilerParams(vmem_limit_bytes=limit),
        cost_estimate=pl.CostEstimate(flops=flops, bytes_accessed=moved, transcendentals=0),
    )(*args)


def trade(blocks):
    count = lax.axis_size(AXES)
    arrived = []
    for block, (step, forward) in zip(blocks, ((PATCH_COLS, 0), (PATCH_COLS, 1), (1, 0), (1, 1))):
        pairs = [
            (p, (p + (step if p // step % 2 != forward else -step)) % count) for p in range(count)
        ]
        arrived.append(lax.ppermute(block, AXES, pairs))
    return arrived


def other_core(value):
    return lax.ppermute(value, "core", [(0, 1), (1, 0)])


def exchange(value):
    chips = lax.axis_size(CHIP)
    blocks = value.reshape(chips, 8, LANES)
    return lax.all_to_all(blocks, CHIP, 0, 0, tiled=True).reshape(chips * 8, LANES)


def shards(
    node_feats,
    edge_feats,
    senders,
    receivers,
    halo_send,
    edge_first,
    edge_second,
    edge_gain,
    node_first,
    node_second,
    node_gain,
    node_cotangent,
    edge_cotangent,
):
    nodes, edges = node_feats.shape[0], edge_feats.shape[0]
    size, blocks = nodes // 4, edges // BLOCK
    devices, chips = lax.axis_size(AXES), lax.axis_size(CHIP)
    coarse_rows = COARSE_DEV * devices
    send, recv = senders.reshape(-1, LANES), receivers.reshape(-1, LANES)
    halo_ids = halo_send.reshape(-1, LANES)
    gain, node_gain = edge_gain[None], node_gain[None]

    spread, *picked = call(
        prepare_kernel,
        [((chips * 8, LANES), BF)] + [((size, D), BF)] * 4,
        (halo_ids, node_feats),
        [pltpu.VMEM((nodes, D), BF)],
        flops=2 * nodes * nodes * D,
    )
    coarse = exchange(spread)
    halos = trade(picked)
    (partial,) = call(
        partial_kernel,
        [((edges, D), F32)],
        (send, recv, edge_feats, node_feats, edge_first),
        [
            pltpu.VMEM((edges, D), BF),
            pltpu.VMEM((nodes, D), BF),
            pltpu.VMEM((3 * D, D), BF),
            pltpu.VMEM((edges, D), F32),
            pltpu.VMEM((2 * nodes, D), BF),
            pltpu.SemaphoreType.DMA((4,)),
            pltpu.SemaphoreType.DMA((edges // STREAM,)),
            pltpu.SemaphoreType.DMA((edges // STREAM, PARTS)),
        ],
        flops=2 * edges * D * (D + 2 * nodes),
        specs={2: ANY, 3: ANY, 4: ANY},
        out_specs={0: ANY},
    )
    coarse, partial, *halos = lax.optimization_barrier((coarse, partial, *halos))
    coarse_other = other_core(coarse)
    edge_out, hidden_bar, node_out, keep, away, node_acc, *grads = call(
        main_kernel,
        [
            ((edges, D), BF),
            ((edges, D), BF),
            ((nodes, D), BF),
            ((chips * 8, LANES), BF),
            ((chips * 8, LANES), BF),
            ((nodes, D), F32),
        ]
        + [((size, D), BF)] * 4,
        (
            send,
            recv,
            gain,
            node_gain,
            partial,
            edge_feats,
            edge_cotangent,
            node_feats,
            node_cotangent,
            *halos,
            coarse,
            coarse_other,
            edge_first,
            edge_second,
            node_first,
            node_second,
        ),
        [
            pltpu.VMEM((edges, D), F32),
            pltpu.VMEM((edges, D), BF),
            pltpu.VMEM((edges, D), BF),
            pltpu.VMEM((nodes, D), BF),
            pltpu.VMEM((nodes, D), BF),
            pltpu.VMEM((nodes, D), BF),
            pltpu.VMEM((2 * chips * 8, LANES), BF),
            pltpu.VMEM((2 * D, D), BF),
            pltpu.VMEM((D, D), BF),
            pltpu.VMEM((2 * D, D), BF),
            pltpu.VMEM((D, D), BF),
            pltpu.VMEM((edges, D), BF),
            pltpu.VMEM((edges, D), BF),
            pltpu.VMEM((nodes + coarse_rows, D), BF),
            pltpu.VMEM((2 * chips * 8, LANES), F32),
            pltpu.VMEM((edges, D), F32),
            pltpu.VMEM((edges, 1), F32),
            pltpu.VMEM((nodes, D), F32),
            pltpu.VMEM((nodes, D), BF),
            pltpu.VMEM((chips * 8, LANES), BF),
            pltpu.VMEM((chips * 8, LANES), BF),
            pltpu.VMEM((nodes, D), F32),
            pltpu.SemaphoreType.DMA((5, blocks)),
            pltpu.SemaphoreType.DMA((13,)),
            pltpu.SemaphoreType.DMA((8,)),
        ],
        flops=2 * edges * D * (2 * coarse_rows + 5 * nodes + 2 * D),
        specs={i: ANY for i in range(4, 19)},
        out_specs={i: ANY for i in range(10)},
    )
    (edge_grads,) = call(
        edge_grads_kernel,
        [((edges, D), BF)],
        (hidden_bar, edge_cotangent, edge_first),
        [
            pltpu.VMEM((edges, D), BF),
            pltpu.VMEM((edges, D), BF),
            pltpu.VMEM((D, D), BF),
            pltpu.VMEM((edges, D), BF),
            pltpu.SemaphoreType.DMA((1,)),
            pltpu.SemaphoreType.DMA((edges // STREAM, 2)),
            pltpu.SemaphoreType.DMA((edges // STREAM, PARTS)),
        ],
        flops=2 * edges * D * D,
        specs={0: ANY, 1: ANY, 2: ANY},
        out_specs={0: ANY},
    )
    backs = trade(grads)
    (pair,) = call(
        pair_kernel, [(keep.shape, BF)], (keep, other_core(away)), limit=FINAL_LIMIT
    )
    parts = exchange(pair)
    parts, *backs = lax.optimization_barrier((parts, *backs))
    (node_grads,) = call(
        final_kernel,
        [((nodes, D), BF)],
        (halo_ids, node_acc, *backs, parts),
        [pltpu.VMEM((nodes, D), BF)],
        limit=FINAL_LIMIT,
        flops=2 * nodes * nodes * D,
    )
    return node_out, edge_out, node_grads, edge_grads


def solution(mesh):
    split = mesh.devices.reshape(-1) if mesh.devices.size != 256 else mesh.devices
    shape = (4, 4, 8, 2) if mesh.devices.size == 256 else (1, 1, 1, mesh.devices.size)
    torus = Mesh(split.reshape(shape), AXES)
    rows, vector, whole = P(AXES, None), P(AXES), P()
    in_specs = (rows, rows, vector, vector, vector) + (whole,) * 6 + (rows, rows)
    return jax.shard_map(
        shards, mesh=torus, in_specs=in_specs, out_specs=(rows,) * 4, check_vma=False
    )
```
